32 devices in a mesh: parts: 2 (over y), blk: 16 (over z, x, core).
Axes of the slice: x: 2, y: 2, z: 4, core: 2. Of those that a mesh axis runs over, the one named last changes fastest.
Arguments:
- series: bfloat16 [16, 192, 11264], P(None, None, 'blk'), may hold values from -24 to 24
- subject_ids: int32 [16], P('parts'), parts along dimension 0, may hold values from 0 to 15
- net_labels: int32 [16], replicated, may hold values from 0 to 6
Outputs:
- connectome: float32 [22528, 11264], P(('parts', 'blk')), parts along dimension 0
The draws below stay inside these ranges and needn't reach their ends.
There are 2 independent parts, one for each index of `parts`. The reference program is written for one: setup_inputs(seed, part) draws one part's arguments, and reference() takes and returns one part's arrays. A program takes and returns all parts, laid end to end along the dimension named above; an argument that names none is the same for every part. Nothing has to cross between parts.
Inputs may be any that keep to these rules, and one draw needn't show every extreme that they name: `subject_ids`: indices into the pool; a subject may repeat.
All inputs are finite; a program needn't handle non-finite values.
Results may differ from the reference program's by a relative error of at most 0.00072.
Values may be sent and summed in bfloat16 or wider, within the bound.
No kernel may reach another device: no remote copies, remote signals or barrier semaphores. Data moves between devices by JAX's collectives and lax.ppermute only.
A program may use at most 384 MiB of HBM per device.

```python
import math
import jax
import jax.numpy as jnp
import numpy as np
from jax import lax

BLOCK = 704
NBLOCK = 16
NET = 7
SUBJ = 8
POOL = 16
FRAMES = 192
G = 11264


def draw_series(key, part):
    keys = jax.random.split(key, 4)
    own = jax.random.truncated_normal(keys[0], -4.0, 4.0, (POOL, FRAMES, NBLOCK), jnp.float32)
    common = jax.random.truncated_normal(keys[1], -4.0, 4.0, (POOL, FRAMES, 1), jnp.float32)
    latent = jnp.repeat(own + 0.7 * common, BLOCK, axis=2)
    loading = jax.random.uniform(keys[2], (POOL, 1, G), jnp.float32, 0.8, 2.5)
    noise = jax.random.truncated_normal(keys[3], -4.0, 4.0, (POOL, FRAMES, G), jnp.float32)
    values = loading * latent + noise
    return values.astype(jnp.bfloat16)


def with_ends(values, key, least, largest):
    extent = values.shape
    place = [jax.random.randint(jax.random.fold_in(key, axis), (), 0, extent[axis]) for axis in range(len(extent))]
    values = values.at[tuple(place)].set(least)
    longest = extent.index(max(extent))
    place[longest] = (place[longest] + 1) % extent[longest]
    return values.at[tuple(place)].set(largest)


def rank_bounds(count, lean):
    portions = [(1 << 20) // math.isqrt(standing ** lean) + 1 for standing in range(1, count + 1)]
    scale = 1 + sum(portions) // (1 << 30)
    return np.cumsum(np.array([max(1, weight // scale) for weight in portions]))


def skewed_ids(stream_key, shape, count, skew):
    grid = rank_bounds(count, skew)
    pick = jax.random.randint(jax.random.fold_in(stream_key, 1), shape, 0, int(grid[count - 1]))
    rank = jnp.searchsorted(jnp.asarray(grid, jnp.int32), pick, side="right")
    return jax.random.permutation(jax.random.fold_in(stream_key, 2), count)[rank].astype(jnp.int32)


def setup_inputs(seed: int = 0, part: int = 0) -> dict:
    streams_of = jax.random.split(jax.random.key(seed), 4)
    part_keys = jax.random.split(jax.random.fold_in(streams_of[3], part), 4)
    return {
        "series": draw_series(jax.random.fold_in(streams_of[3], 71), part),
        "subject_ids": with_ends(jax.random.randint(part_keys[1], (SUBJ,), 0, POOL), jax.random.fold_in(part_keys[1], 1), 0, POOL - 1).astype(jnp.int32),
        "net_labels": with_ends(skewed_ids(streams_of[2], (NBLOCK,), NET, 2), jax.random.fold_in(streams_of[2], 3), 0, NET - 1).astype(jnp.int32),
    }


def fisher_value(corr):
    clipped = jnp.clip(corr, -0.999, 0.999)
    return 0.5 * jnp.log((1.0 + clipped) / (1.0 - clipped))

def reference(series, subject_ids, net_labels):
    chosen = series[subject_ids].astype(jnp.float32)
    center = chosen - lax.optimization_barrier(jnp.mean(chosen, axis=1, keepdims=True))
    spread = lax.optimization_barrier(jnp.mean(center * center, axis=1, keepdims=True))
    normalized = (center / jnp.sqrt(spread + 1e-05)).astype(jnp.bfloat16)
    row_labels = jnp.repeat(net_labels, BLOCK)
    blocks = normalized.reshape(SUBJ, FRAMES, NBLOCK, BLOCK).transpose(2, 0, 1, 3)

    def one_block(inputs):
        block_rows, label = inputs
        total = jnp.zeros((BLOCK, G), jnp.float32)
        for subject in range(SUBJ):
            corr = jnp.dot(block_rows[subject].T, normalized[subject], preferred_element_type=jnp.float32) / FRAMES
            total = total + fisher_value(corr)
        return jnp.where(label == row_labels[None, :], total, jnp.zeros_like(total))
    result = lax.map(one_block, (blocks, net_labels))
    return result.reshape(G, G)
```

```python
import functools

import jax
import jax.numpy as jnp
from jax import lax
from jax.experimental import pallas as pl
from jax.experimental.pallas import tpu as pltpu
from jax.sharding import PartitionSpec as P

CLIP = 0.999
EPS = 1e-05
VMEM = 56 * 2**20


def plans(subjects):
    least = subjects * 5 // 8
    out = [(n, m) for n in range(least, subjects) for m in range(1, subjects - n + 1)]
    return out + [(subjects, 0)]


def table_kernel(me_ref, own_ref, other_ref, plan_ref, slots_ref, where_ref, fetch, place):
    subjects = own_ref.shape[0]
    pool = place.shape[1]
    me = me_ref[0]
    one = jnp.int32(1)
    own = jnp.int32(0)
    other = jnp.int32(0)
    for s in range(subjects):
        own = own | (one << own_ref[s])
        other = other | (one << other_ref[s])
    has = (jnp.where(me == 0, own, other), jnp.where(me == 0, other, own))
    both = has[0] & has[1]

    def count(mask):
        total = jnp.int32(0)
        for u in range(pool):
            total = total + ((mask >> u) & 1)
        return total

    distinct = (count(has[0]), count(has[1]))
    common = count(both)
    n = jnp.int32(subjects)
    for cand in range(subjects - 1, subjects * 5 // 8 - 1, -1):
        short = jnp.maximum(distinct[0] - cand, 0) + jnp.maximum(distinct[1] - cand, 0)
        n = jnp.where(jnp.logical_and(n == cand + 1, short <= common), cand, n)
    taken = (jnp.maximum(distinct[0] - n, 0), jnp.maximum(distinct[1] - n, 0))
    m = jnp.maximum(jnp.maximum(taken[0], taken[1]), 1)
    plan = jnp.int32(0)
    for i, (a, b) in enumerate(plans(subjects)):
        hit = n == a if b == 0 else jnp.logical_and(n == a, m == b)
        plan = jnp.where(hit, i, plan)
    plan_ref[0] = plan

    take = [jnp.int32(0), jnp.int32(0)]
    seen = jnp.int32(0)
    for u in range(pool):
        bit = (both >> u) & 1
        first = jnp.where(seen < taken[0], bit, 0)
        second = jnp.where(jnp.logical_and(seen >= taken[0], seen < taken[0] + taken[1]), bit, 0)
        take[0] = take[0] | (first << u)
        take[1] = take[1] | (second << u)
        seen = seen + bit
    for p in range(2):
        for k in range(subjects):
            fetch[p, k] = 0
        ahead = jnp.int32(0)
        behind = taken[1 - p]
        for u in range(pool):
            give = (take[1 - p] >> u) & 1
            keep = (((has[p] & ~take[p]) >> u) & 1) * (1 - give)
            spot = jnp.where(give == 1, ahead, behind)
            place[p, u] = spot

            @pl.when(give + keep == 1)
            def _():
                fetch[p, spot] = u

            ahead = ahead + give
            behind = behind + keep
    mine = jnp.where(me == 0, take[0], take[1])
    for k in range(subjects):
        slots_ref[k] = jnp.where(k < n, fetch[me, k], fetch[1 - me, jnp.maximum(k - n, 0)])
    for s in range(subjects):
        u = own_ref[s]
        from_other = ((mine >> u) & 1) == 1
        where_ref[s] = jnp.where(from_other, n + place[1 - me, u], place[me, u])


def tables(me, own, other, pool):
    subjects = own.shape[0]
    smem = pl.BlockSpec(memory_space=pltpu.SMEM)
    return pl.pallas_call(
        table_kernel,
        in_specs=[smem] * 3,
        out_specs=[smem] * 3,
        out_shape=[
            jax.ShapeDtypeStruct((1,), jnp.int32),
            jax.ShapeDtypeStruct((subjects,), jnp.int32),
            jax.ShapeDtypeStruct((subjects,), jnp.int32),
        ],
        scratch_shapes=[
            pltpu.SMEM((2, subjects), jnp.int32),
            pltpu.SMEM((2, pool), jnp.int32),
        ],
    )(me, own, other)


def normalize_kernel(slots_ref, series_ref, out_ref):
    values = series_ref[...].astype(jnp.float32)
    center = values - jnp.mean(values, axis=0, keepdims=True)
    spread = jnp.mean(center * center, axis=0, keepdims=True)
    out_ref[...] = (center / jnp.sqrt(spread + EPS)).astype(jnp.bfloat16)


def normalize_slots(series, slots, first, last):
    _, frames, rows = series.shape
    grid_spec = pltpu.PrefetchScalarGridSpec(
        num_scalar_prefetch=1,
        grid=(last - first,),
        in_specs=[pl.BlockSpec((None, frames, rows), lambda i, slots: (slots[i + first], 0, 0))],
        out_specs=pl.BlockSpec((None, frames, rows), lambda i, slots: (i, 0, 0)),
    )
    return pl.pallas_call(
        normalize_kernel,
        grid_spec=grid_spec,
        out_shape=jax.ShapeDtypeStruct((last - first, frames, rows), jnp.bfloat16),
        cost_estimate=pl.CostEstimate(
            flops=8 * (last - first) * frames * rows,
            bytes_accessed=4 * (last - first) * frames * rows,
            transcendentals=0,
        ),
    )(slots, series)


def fisher_kernel(
    parts, codes, step, me_ref, labels_ref, where_ref, left_ref, *refs
):
    count = len(codes)
    spans = [k for k in parts if k]
    kinds = len(spans)
    sources = [refs[e * kinds : (e + 1) * kinds] for e in range(2 * count)]
    out_ref, buffer, tile, blank, todo, fetch_sem, tile_sem, blank_sem = refs[2 * count * kinds :]
    _, rows, frames = left_ref.shape
    width = buffer.shape[3]
    subjects = where_ref.shape[0]
    me = me_ref[0]
    core = me & 1
    label = labels_ref[me]
    scale = jnp.float32(frames)
    limit = jnp.float32(CLIP * frames)

    starts = [sum(spans[:k]) for k in range(kinds)]

    def pair_of(code):
        return (me >> 1) ^ code

    def fetch_copies(e, slot):
        return [
            pltpu.make_async_copy(
                sources[e][k], buffer.at[slot, pl.ds(starts[k], spans[k])], fetch_sem.at[slot, k]
            )
            for k in range(kinds)
        ]

    def blank_copy(j):
        column = pl.multiple_of(pair_of(codes[j]) * (2 * width), 128)
        return pltpu.make_async_copy(blank, out_ref.at[:, pl.ds(column, 2 * width)], blank_sem.at[j])

    wanted = []
    total = jnp.int32(0)
    for j, code in enumerate(codes):
        pair = pair_of(code)
        for h in range(2):
            hit = labels_ref[2 * pair + h] == label
            wanted.append(hit)
            todo[total] = 2 * j + h
            total = total + jnp.where(hit, 1, 0)
    empty = [jnp.logical_not(jnp.logical_or(wanted[2 * j], wanted[2 * j + 1])) for j in range(count)]

    def start_fetch(i, slot):
        item = todo[i]
        h = item & 1
        entry = (item & ~1) | jnp.where(h == core, 0, 1)
        for e in range(2 * count):

            @pl.when(entry == e)
            def _():
                for copy in fetch_copies(e, slot):
                    copy.start()

    @pl.when(total > 0)
    def _():
        start_fetch(0, 0)

    blank[...] = jnp.zeros_like(blank)
    for j in range(count):

        @pl.when(empty[j])
        def _():
            blank_copy(j).start()

    def tile_copy(pair, slot):
        column = pl.multiple_of(pair * (2 * width), 128)
        return pltpu.make_async_copy(tile.at[slot], out_ref.at[:, pl.ds(column, 2 * width)], tile_sem.at[slot])

    def code_of(j):
        code = jnp.int32(codes[0])
        for k in range(1, count):
            code = jnp.where(j == k, codes[k], code)
        return code

    chunk = min(256, width)

    def body(i, pairs):
        slot = i % 2
        item = todo[i]
        j = item >> 1
        h = item & 1
        opens = jnp.logical_or(i == 0, (todo[jnp.maximum(i - 1, 0)] >> 1) != j)
        closes = jnp.logical_or(i == total - 1, (todo[jnp.minimum(i + 1, total - 1)] >> 1) != j)
        pairs = pairs + jnp.where(opens, 1, 0)
        spot = pairs % 2

        @pl.when(i + 1 < total)
        def _():
            start_fetch(i + 1, 1 - slot)

        @pl.when(jnp.logical_and(opens, pairs > 2))
        def _():
            tile_copy(0, spot).wait()

        @pl.when(jnp.logical_and(opens, closes))
        def _():
            tile[spot] = jnp.zeros(tile.shape[1:], jnp.float32)

        for copy in fetch_copies(0, slot):
            copy.wait()

        for half in range(2):

            @pl.when(h == half)
            def _():
                @pl.loop(0, rows // step)
                def _(r):
                    band = pl.ds(pl.multiple_of(r * step, 16), step)
                    for low in range(0, width, chunk):
                        high = min(low + chunk, width)
                        up = down = None
                        for s in range(subjects):
                            k = where_ref[s]
                            corr = jnp.dot(
                                left_ref[k, band, :],
                                buffer[slot, k, :, low:high],
                                preferred_element_type=jnp.float32,
                            )
                            corr = jnp.clip(corr, -limit, limit)
                            plus, minus = scale + corr, scale - corr
                            up = plus if up is None else up * plus
                            down = minus if down is None else down * minus
                        tile[spot, band, half * width + low : half * width + high] = 0.5 * jnp.log(up / down)

        @pl.when(closes)
        def _():
            tile_copy(pair_of(code_of(j)), spot).start()

        return pairs

    pairs = lax.fori_loop(0, total, body, jnp.int32(0))

    @pl.when(pairs > 0)
    def _():
        tile_copy(0, pairs % 2).wait()

    @pl.when(pairs > 1)
    def _():
        tile_copy(0, (pairs + 1) % 2).wait()

    for j in range(count):

        @pl.when(empty[j])
        def _():
            blank_copy(j).wait()


def band_rows(rows):
    return next(k for k in range(min(rows, 192), 0, -1) if rows % k == 0 and (k % 16 == 0 or k == rows))


def fisher(me, labels, where, left, pairs, codes, parts, out=None):
    slots, rows, frames = left.shape
    width = rows
    columns = labels.shape[0] * width
    any_spec = pl.BlockSpec(memory_space=pl.ANY)
    smem = pl.BlockSpec(memory_space=pltpu.SMEM)
    arrays = [x for pair in pairs for side in pair for x in side]
    kinds = len([k for k in parts if k])
    count = len(codes)
    blocks = 2 * count
    step = band_rows(rows)
    return pl.pallas_call(
        functools.partial(fisher_kernel, parts, codes, step),
        in_specs=[smem, smem, smem, pl.BlockSpec(memory_space=pltpu.VMEM)] + [any_spec] * len(arrays),
        out_specs=any_spec,
        out_shape=jax.ShapeDtypeStruct((rows, columns), jnp.float32),
        scratch_shapes=[
            pltpu.VMEM((2, slots, frames, width), jnp.bfloat16),
            pltpu.VMEM((2, rows, 2 * width), jnp.float32),
            pltpu.VMEM((rows, 2 * width), jnp.float32),
            pltpu.SMEM((blocks + 1,), jnp.int32),
            pltpu.SemaphoreType.DMA((2, kinds)),
            pltpu.SemaphoreType.DMA((2,)),
            pltpu.SemaphoreType.DMA((count,)),
        ],
        compiler_params=pltpu.CompilerParams(vmem_limit_bytes=VMEM),
        cost_estimate=pl.CostEstimate(
            flops=2 * rows * width * frames * slots * blocks // 2,
            bytes_accessed=rows * columns * 4,
            transcendentals=rows * width * blocks // 2,
        ),
    )(me, labels, where, left, *arrays)


def fast(series, subject_ids, net_labels, blocks):
    pool = series.shape[0]
    subjects = subject_ids.shape[0]
    index = lax.axis_index("blk").astype(jnp.int32)
    part = lax.axis_index("parts").astype(jnp.int32)
    other = lax.ppermute(subject_ids, "parts", [(0, 1), (1, 0)])
    plan, slots, where = tables(part[None], subject_ids, other, pool)

    def plane(k):
        return k >> 2

    last = plane(blocks - 1)
    inner = [i for i in range(blocks) if 0 < plane(i) < last]
    swap_core = [(i, i ^ 1) for i in range(blocks)]
    swap_x = [(i, i ^ 2) for i in range(blocks)]
    swap_z = [(i, i ^ 4) for i in range(blocks)]
    swap_mid = [(i, i ^ 12) for i in inner]
    outward = [(i, i ^ 4) for i in inner]
    at_end = jnp.logical_or(index >> 2 == 0, index >> 2 == last)

    def send(x, perm):
        return lax.ppermute(x, "blk", perm)

    def route(own, tail):
        r1, mid, x0 = send(own, swap_z), send(own, swap_mid), send(own, swap_x)
        x1 = send(r1, swap_x)
        r2 = jnp.where(at_end, send(mid, outward), send(r1, swap_mid))
        x2 = send(r2, swap_x)
        r3 = jnp.where(at_end, send(r2, outward), mid)
        if tail == "x":
            x3 = send(r3, swap_x)
        else:
            x3 = jnp.where(at_end, send(x2, outward), send(x0, swap_mid))
        return [r1, x0, r2, x1, r3, x2, x3]

    codes = (0, 2, 1, 4, 3, 6, 5, 7)

    def branch(n, m):
        def run(series, slots, where, net_labels):
            if m:
                spans = [
                    normalize_slots(series, slots, 0, m),
                    normalize_slots(series, slots, m, n),
                    normalize_slots(series, slots, n, n + m),
                ]
                first = route(spans[0], "x")
                second = route(spans[1], "z")
                third = [lax.ppermute(x, "parts", [(0, 1), (1, 0)]) for x in first]
                sides = [spans] + [list(k) for k in zip(first, second, third)]
            else:
                half = n // 2
                spans = [normalize_slots(series, slots, 0, half), normalize_slots(series, slots, half, n)]
                sides = [spans] + [list(k) for k in zip(route(spans[0], "x"), route(spans[1], "z"))]
            parts = [x.shape[0] for x in spans]
            left = jnp.swapaxes(jnp.concatenate(spans, axis=0), 1, 2)
            pairs = [(side, [send(x, swap_core) for x in side]) for side in sides]
            return fisher(index[None], net_labels, where, left, pairs, codes, parts)

        return run

    return lax.switch(
        plan[0], [branch(n, m) for n, m in plans(subjects)], series, slots, where, net_labels
    )


def general(series, subject_ids, net_labels, block):
    chosen = jnp.take(series, subject_ids, axis=0).astype(jnp.float32)
    center = chosen - jnp.mean(chosen, axis=1, keepdims=True)
    spread = jnp.mean(center * center, axis=1, keepdims=True)
    left = (center / jnp.sqrt(spread + EPS)).astype(jnp.bfloat16)
    subjects, frames, rows = left.shape
    right = lax.all_gather(left, "blk", axis=2, tiled=True)
    row_labels = jnp.repeat(net_labels, block)
    own_labels = lax.dynamic_slice_in_dim(row_labels, lax.axis_index("blk") * rows, rows)
    up = down = jnp.float32(1)
    for s in range(subjects):
        corr = lax.dot_general(
            left[s], right[s], (((0,), (0,)), ((), ())), preferred_element_type=jnp.float32
        )
        corr = jnp.clip(corr / frames, -CLIP, CLIP)
        up, down = up * (1 + corr), down * (1 - corr)
    total = 0.5 * jnp.log(up / down)
    return jnp.where(own_labels[:, None] == row_labels[None, :], total, jnp.zeros_like(total))


def solution(mesh):
    parts, devices = mesh.shape["parts"], mesh.shape["blk"]

    def on_device(series, subject_ids, net_labels):
        blocks = net_labels.shape[0]
        rows = series.shape[2]
        grid = 4 * 2 * 2
        if parts == 2 and devices == blocks == grid and 2 * rows % 128 == 0:
            return fast(series, subject_ids, net_labels, blocks)
        return general(series, subject_ids, net_labels, rows * devices // blocks)

    return jax.shard_map(
        on_device,
        mesh=mesh,
        in_specs=(P(None, None, "blk"), P("parts"), P()),
        out_specs=P(("parts", "blk"), None),
        check_vma=False,
    )
```

```python
import functools

import jax
import jax.numpy as jnp
from jax import lax
from jax.experimental import pallas as pl
from jax.experimental.pallas import tpu as pltpu
from jax.sharding import PartitionSpec as P

CLIP = 0.999
EPS = 1e-05
VMEM = 56 * 2**20


def plans(subjects):
    n = subjects * 5 // 8
    return [(n, subjects - n - 1), (n + 1, subjects - n - 1), (subjects, 0)]


def table_kernel(me_ref, own_ref, other_ref, plan_ref, slots_ref, where_ref, fetch, place):
    subjects = own_ref.shape[0]
    pool = place.shape[1]
    me = me_ref[0]
    one = jnp.int32(1)
    own = jnp.int32(0)
    other = jnp.int32(0)
    for s in range(subjects):
        own = own | (one << own_ref[s])
        other = other | (one << other_ref[s])
    has = (jnp.where(me == 0, own, other), jnp.where(me == 0, other, own))
    both = has[0] & has[1]

    def count(mask):
        total = jnp.int32(0)
        for u in range(pool):
            total = total + ((mask >> u) & 1)
        return total

    distinct = (count(has[0]), count(has[1]))
    common = count(both)
    n = jnp.int32(subjects)
    plan = jnp.int32(0)
    for i, (cand, most) in reversed(list(enumerate(plans(subjects)))):
        short = [jnp.maximum(d - cand, 0) for d in distinct]
        fits = jnp.logical_and(short[0] + short[1] <= common, jnp.maximum(short[0], short[1]) <= most)
        n = jnp.where(fits, cand, n)
        plan = jnp.where(fits, i, plan)
    taken = (jnp.maximum(distinct[0] - n, 0), jnp.maximum(distinct[1] - n, 0))
    plan_ref[0] = plan

    take = [jnp.int32(0), jnp.int32(0)]
    seen = jnp.int32(0)
    for u in range(pool):
        bit = (both >> u) & 1
        first = jnp.where(seen < taken[0], bit, 0)
        second = jnp.where(jnp.logical_and(seen >= taken[0], seen < taken[0] + taken[1]), bit, 0)
        take[0] = take[0] | (first << u)
        take[1] = take[1] | (second << u)
        seen = seen + bit
    for p in range(2):
        for k in range(subjects):
            fetch[p, k] = 0
        ahead = jnp.int32(0)
        behind = taken[1 - p]
        for u in range(pool):
            give = (take[1 - p] >> u) & 1
            keep = (((has[p] & ~take[p]) >> u) & 1) * (1 - give)
            spot = jnp.where(give == 1, ahead, behind)
            place[p, u] = spot

            @pl.when(give + keep == 1)
            def _():
                fetch[p, spot] = u

            ahead = ahead + give
            behind = behind + keep
    mine = jnp.where(me == 0, take[0], take[1])
    for k in range(subjects):
        slots_ref[k] = jnp.where(k < n, fetch[me, k], fetch[1 - me, jnp.maximum(k - n, 0)])
    for s in range(subjects):
        u = own_ref[s]
        from_other = ((mine >> u) & 1) == 1
        where_ref[s] = jnp.where(from_other, n + place[1 - me, u], place[me, u])


def tables(me, own, other, pool):
    subjects = own.shape[0]
    smem = pl.BlockSpec(memory_space=pltpu.SMEM)
    return pl.pallas_call(
        table_kernel,
        in_specs=[smem] * 3,
        out_specs=[smem] * 3,
        out_shape=[
            jax.ShapeDtypeStruct((1,), jnp.int32),
            jax.ShapeDtypeStruct((subjects,), jnp.int32),
            jax.ShapeDtypeStruct((subjects,), jnp.int32),
        ],
        scratch_shapes=[
            pltpu.SMEM((2, subjects), jnp.int32),
            pltpu.SMEM((2, pool), jnp.int32),
        ],
    )(me, own, other)


def normalize_kernel(first, turned, slots_ref, series_ref, out_ref, held, done, sem):
    count = held.shape[0]

    def load(i):
        return pltpu.make_async_copy(series_ref.at[slots_ref[first + i]], held.at[i], sem.at[0, i])

    def store(i):
        return pltpu.make_async_copy(done.at[i], out_ref.at[i], sem.at[1, i])

    for i in range(count):
        load(i).start()

    @pl.loop(0, count)
    def _(i):
        load(i).wait()
        values = held[i].astype(jnp.float32)
        center = values - jnp.mean(values, axis=0, keepdims=True)
        spread = jnp.mean(center * center, axis=0, keepdims=True)
        value = center * (1 / jnp.sqrt(spread + EPS))
        done[i] = (value.T if turned else value).astype(jnp.bfloat16)
        store(i).start()

    for i in range(count):
        store(i).wait()


def normalize_slots(series, slots, first, last, turned=False):
    _, frames, rows = series.shape
    shape = (rows, frames) if turned else (frames, rows)
    count = last - first
    any_spec = pl.BlockSpec(memory_space=pl.ANY)
    return pl.pallas_call(
        functools.partial(normalize_kernel, first, turned),
        in_specs=[pl.BlockSpec(memory_space=pltpu.SMEM), any_spec],
        out_specs=any_spec,
        out_shape=jax.ShapeDtypeStruct((count, *shape), jnp.bfloat16),
        scratch_shapes=[
            pltpu.VMEM((count, frames, rows), jnp.bfloat16),
            pltpu.VMEM((count, *shape), jnp.bfloat16),
            pltpu.SemaphoreType.DMA((2, count)),
        ],
        compiler_params=pltpu.CompilerParams(vmem_limit_bytes=VMEM),
        cost_estimate=pl.CostEstimate(
            flops=8 * count * frames * rows,
            bytes_accessed=4 * count * frames * rows,
            transcendentals=0,
        ),
    )(slots, series)


def fisher_kernel(codes, blanks, entries, arrays, has_prev, step, *refs):
    me_ref, labels_ref, where_ref, left_hbm = refs[:4]
    sources = refs[4 : 4 + arrays]
    out_ref, left_ref, buffer, half_ref, tile, blank, todo, left_sem, fetch_sem, tile_sem, blank_sem = refs[
        4 + arrays + has_prev :
    ]
    count = len(codes)
    _, rows, frames = left_ref.shape
    width = buffer.shape[3]
    subjects = where_ref.shape[0]
    me = me_ref[0]
    core = me & 1
    label = labels_ref[me]
    scale = jnp.float32(frames)
    limit = jnp.float32(CLIP * frames)

    def pair_of(code):
        return (me >> 1) ^ code

    def columns(pair):
        return out_ref.at[:, pl.ds(pl.multiple_of(pair * (2 * width), 128), 2 * width)]

    total = jnp.int32(0)
    for j, code in enumerate(codes):
        for h in range(2):
            todo[total] = 2 * j + h
            total = total + jnp.where(labels_ref[2 * pair_of(code) + h] == label, 1, 0)

    def start_fetch(i, slot):
        item = todo[i]
        entry = (item & ~1) | jnp.where((item & 1) == core, 0, 1)
        for e, pieces in enumerate(entries):

            @pl.when(entry == e)
            def _():
                at = 0
                for array, first, span in pieces:
                    pltpu.make_async_copy(
                        sources[array].at[pl.ds(first, span)], buffer.at[slot, pl.ds(at, span)], fetch_sem.at[slot]
                    ).start()
                    at += span

    left_copy = pltpu.make_async_copy(left_hbm, left_ref, left_sem.at[0])

    @pl.when(total > 0)
    def _():
        left_copy.start()
        start_fetch(0, 0)

    if blanks:
        blank[...] = jnp.zeros_like(blank)
    empty = []
    for j, code in enumerate(blanks):
        pair = pair_of(code)
        unwanted = jnp.logical_and(labels_ref[2 * pair] != label, labels_ref[2 * pair + 1] != label)
        empty.append((unwanted, pltpu.make_async_copy(blank, columns(pair), blank_sem.at[j])))

        @pl.when(unwanted)
        def _(j=j):
            empty[j][1].start()

    def tile_copy(pair, slot):
        return pltpu.make_async_copy(tile.at[slot], columns(pair), tile_sem.at[slot])

    def code_of(j):
        code = jnp.int32(codes[0])
        for k in range(1, count):
            code = jnp.where(j == k, codes[k], code)
        return code

    chunk = min(256, width)

    @pl.when(total > 0)
    def _():
        left_copy.wait()

    def body(i, pairs):
        slot = i % 2
        item = todo[i]
        j = item >> 1
        h = item & 1
        opens = jnp.logical_or(i == 0, (todo[jnp.maximum(i - 1, 0)] >> 1) != j)
        closes = jnp.logical_or(i == total - 1, (todo[jnp.minimum(i + 1, total - 1)] >> 1) != j)
        pairs = pairs + jnp.where(opens, 1, 0)
        spot = pairs % 2

        @pl.when(i + 1 < total)
        def _():
            start_fetch(i + 1, 1 - slot)

        @pl.when(jnp.logical_and(opens, pairs > 2))
        def _():
            tile_copy(0, spot).wait()

        @pl.when(jnp.logical_and(opens, closes))
        def _():
            tile[spot] = jnp.zeros(tile.shape[1:], jnp.float32)

        pltpu.make_async_copy(buffer.at[slot], buffer.at[slot], fetch_sem.at[slot]).wait()

        @pl.loop(0, rows // step)
        def _(r):
            band = pl.ds(pl.multiple_of(r * step, 16), step)
            for low in range(0, width, chunk):
                high = min(low + chunk, width)
                up = down = None
                for s in range(subjects):
                    k = where_ref[s]
                    corr = jnp.dot(
                        left_ref[k, band, :], buffer[slot, k, :, low:high], preferred_element_type=jnp.float32
                    )
                    corr = jnp.clip(corr, -limit, limit)
                    plus, minus = scale + corr, scale - corr
                    up = plus if up is None else up * plus
                    down = minus if down is None else down * minus
                half_ref[band, low:high] = 0.5 * jnp.log(up / down)

        for half in range(2):

            @pl.when(h == half)
            def _():
                tile[spot, :, half * width : (half + 1) * width] = half_ref[...]

        @pl.when(closes)
        def _():
            tile_copy(pair_of(code_of(j)), spot).start()

        return pairs

    pairs = lax.fori_loop(0, total, body, jnp.int32(0))

    @pl.when(pairs > 0)
    def _():
        tile_copy(0, pairs % 2).wait()

    @pl.when(pairs > 1)
    def _():
        tile_copy(0, (pairs + 1) % 2).wait()

    for unwanted, copy in empty:

        @pl.when(unwanted)
        def _():
            copy.wait()


def band_rows(rows):
    return next(k for k in range(min(rows, 384), 0, -1) if rows % k == 0 and (k % 16 == 0 or k == rows))


def fisher(me, labels, where, left, pairs, blanks=(), prev=None):
    slots, rows, frames = left.shape
    width = rows
    any_spec = pl.BlockSpec(memory_space=pl.ANY)
    smem = pl.BlockSpec(memory_space=pltpu.SMEM)
    arrays, entries = [], []
    for _, *sides in pairs:
        for side in sides:
            entry = []
            for array, first, span in side:
                known = [k for k, x in enumerate(arrays) if x is array]
                if not known:
                    arrays.append(array)
                    known = [len(arrays) - 1]
                entry.append((known[0], first, span))
            entries.append(entry)
    operands = [me, labels, where, left, *arrays] + ([] if prev is None else [prev])
    codes = [pair[0] for pair in pairs]
    return pl.pallas_call(
        functools.partial(
            fisher_kernel, codes, blanks, entries, len(arrays), int(prev is not None), band_rows(rows)
        ),
        in_specs=[smem] * 3 + [any_spec] * (len(operands) - 3),
        out_specs=any_spec,
        out_shape=jax.ShapeDtypeStruct((rows, labels.shape[0] * width), jnp.float32),
        scratch_shapes=[
            pltpu.VMEM((slots, rows, frames), jnp.bfloat16),
            pltpu.VMEM((2, slots, frames, width), jnp.bfloat16),
            pltpu.VMEM((rows, width), jnp.float32),
            pltpu.VMEM((2, rows, 2 * width), jnp.float32),
            pltpu.VMEM((rows, 2 * width), jnp.float32),
            pltpu.SMEM((2 * len(codes) + 1,), jnp.int32),
            pltpu.SemaphoreType.DMA((1,)),
            pltpu.SemaphoreType.DMA((2,)),
            pltpu.SemaphoreType.DMA((2,)),
            pltpu.SemaphoreType.DMA((max(len(blanks), 1),)),
        ],
        input_output_aliases={} if prev is None else {len(operands) - 1: 0},
        compiler_params=pltpu.CompilerParams(vmem_limit_bytes=VMEM),
        cost_estimate=pl.CostEstimate(
            flops=2 * rows * width * frames * slots * len(codes),
            bytes_accessed=rows * width * 8 * max(len(codes), len(blanks)),
            transcendentals=rows * width * len(codes),
        ),
    )(*operands)


def pack_kernel(spans, *refs):
    sources, out_ref, held, sem = refs[: len(spans)], refs[-3], refs[-2], refs[-1]
    loads, stores, at = [], [], 0
    for k, span in enumerate(spans):
        place = pl.ds(at, span)
        loads.append(pltpu.make_async_copy(sources[k], held.at[place], sem.at[0, k]))
        stores.append(pltpu.make_async_copy(held.at[place], out_ref.at[place], sem.at[1, k]))
        at += span
    for copy in loads:
        copy.start()
    for load, store in zip(loads, stores):
        load.wait()
        store.start()
    for copy in stores:
        copy.wait()


def pack(*arrays):
    spans = [x.shape[0] for x in arrays]
    shape = (sum(spans), *arrays[0].shape[1:])
    size = 2 * shape[0] * shape[1] * shape[2]
    any_spec = pl.BlockSpec(memory_space=pl.ANY)
    return pl.pallas_call(
        functools.partial(pack_kernel, spans),
        in_specs=[any_spec] * len(spans),
        out_specs=any_spec,
        out_shape=jax.ShapeDtypeStruct(shape, arrays[0].dtype),
        scratch_shapes=[pltpu.VMEM(shape, arrays[0].dtype), pltpu.SemaphoreType.DMA((2, len(spans)))],
        compiler_params=pltpu.CompilerParams(vmem_limit_bytes=VMEM),
        cost_estimate=pl.CostEstimate(flops=0, bytes_accessed=2 * size, transcendentals=0),
    )(*arrays)


def fast(series, subject_ids, net_labels, blocks):
    pool = series.shape[0]
    subjects = subject_ids.shape[0]
    index = lax.axis_index("blk").astype(jnp.int32)
    part = lax.axis_index("parts").astype(jnp.int32)
    other = lax.ppermute(subject_ids, "parts", [(0, 1), (1, 0)])
    plan, slots, where = tables(part[None], subject_ids, other, pool)

    last = (blocks - 1) >> 2
    inner = [i for i in range(blocks) if 0 < i >> 2 < last]
    at_end = jnp.logical_or(index >> 2 == 0, index >> 2 == last)

    def sender(perm):
        return lambda x: lax.ppermute(x, "blk", perm)

    core = sender([(i, i ^ 1) for i in range(blocks)])
    along_x = sender([(i, i ^ 2) for i in range(blocks)])
    along_z = sender([(i, i ^ 4) for i in range(blocks)])
    middle = sender([(i, i ^ 12) for i in inner])
    outward = sender([(i, i ^ 4) for i in inner])

    def branch(n, m):
        half = (n + 1) // 2
        together = lax.optimization_barrier

        def along_y(*arrays):
            if not m:
                return None
            return lax.ppermute(jnp.concatenate([x[:m] for x in arrays]), "parts", [(0, 1), (1, 0)])

        def twin(x):
            return None if x is None else core(x)

        def fit(*pieces):
            return [p for p in pieces if p[2]]

        def run(series, slots, where, net_labels):
            step = functools.partial(fisher, index[None], net_labels, where)

            def pair(code, a, y, k, both, y_s):
                return code, fit((a, 0, n), (y, k * m, m)), fit((both, k * n, n), (y_s, k * m, m))

            own = normalize_slots(series, slots, 0, n)
            r1, mid, x0, own_s = along_z(own), middle(own), along_x(own), core(own)
            taken = normalize_slots(series, slots, n, n + m) if m else None
            taken_s = twin(taken)
            left = normalize_slots(series, slots, 0, n + m, turned=True)
            r1, mid, x0, own_s, taken, taken_s, left = together((r1, mid, x0, own_s, taken, taken_s, left))

            e2, b2, x1, y1 = outward(mid), middle(r1), along_x(r1), along_y(r1, x0)
            joint2 = pack(r1, x0)
            out = step(
                left,
                [(0, fit((own, 0, n), (taken, 0, m)), fit((own_s, 0, n), (taken_s, 0, m)))],
                blanks=tuple(range(blocks // 2)),
            )
            r2 = jnp.where(at_end, e2, b2)
            r2, x1, y1, joint2, out = together((r2, x1, y1, joint2, out))

            r3, x2, y2, core2, y1_s = along_z(r2), along_x(r2), along_y(r2, x1), core(joint2), twin(y1)
            joint3 = pack(r2, x1)
            r3, x2, y2, core2, y1_s, joint3 = together((r3, x2, y2, core2, y1_s, joint3))

            x3, rest, y3 = along_x(r3[:half]), along_z(x2[half:]), along_y(r3, x2)
            core3, y2_s = core(joint3), twin(y2)
            joint4 = pack(r3, x2)
            out = step(
                left,
                [pair(2, r1, y1, 0, core2, y1_s), pair(1, x0, y1, 1, core2, y1_s)],
                prev=out,
            )
            rest, x3, y3, core3, y2_s, joint4, out = together((rest, x3, y3, core3, y2_s, joint4, out))

            y4, core4, y3_s, x3_s, rest_s = along_y(x3), core(joint4), twin(y3), core(x3), core(rest)
            out = step(
                left,
                [pair(4, r2, y2, 0, core3, y2_s), pair(3, x1, y2, 1, core3, y2_s)],
                prev=out,
            )
            y4, core4, y3_s, x3_s, rest_s, out = together((y4, core4, y3_s, x3_s, rest_s, out))

            y4_s = twin(y4)
            mine = fit((x3, 0, half), (rest, 0, n - half), (y4, 0, m))
            sibling = fit((x3_s, 0, half), (rest_s, 0, n - half), (y4_s, 0, m))
            return step(
                left,
                [
                    pair(6, r3, y3, 0, core4, y3_s),
                    pair(5, x2, y3, 1, core4, y3_s),
                    (7, mine, sibling),
                ],
                prev=out,
            )

        return run

    return lax.switch(
        plan[0], [branch(n, m) for n, m in plans(subjects)], series, slots, where, net_labels
    )


def general(series, subject_ids, net_labels, block):
    chosen = jnp.take(series, subject_ids, axis=0).astype(jnp.float32)
    center = chosen - jnp.mean(chosen, axis=1, keepdims=True)
    spread = jnp.mean(center * center, axis=1, keepdims=True)
    left = (center / jnp.sqrt(spread + EPS)).astype(jnp.bfloat16)
    subjects, frames, rows = left.shape
    right = lax.all_gather(left, "blk", axis=2, tiled=True)
    row_labels = jnp.repeat(net_labels, block)
    own_labels = lax.dynamic_slice_in_dim(row_labels, lax.axis_index("blk") * rows, rows)
    up = down = jnp.float32(1)
    for s in range(subjects):
        corr = lax.dot_general(
            left[s], right[s], (((0,), (0,)), ((), ())), preferred_element_type=jnp.float32
        )
        corr = jnp.clip(corr / frames, -CLIP, CLIP)
        up, down = up * (1 + corr), down * (1 - corr)
    total = 0.5 * jnp.log(up / down)
    return jnp.where(own_labels[:, None] == row_labels[None, :], total, jnp.zeros_like(total))


def solution(mesh):
    parts, devices = mesh.shape["parts"], mesh.shape["blk"]

    def on_device(series, subject_ids, net_labels):
        blocks = net_labels.shape[0]
        rows = series.shape[2]
        grid = 4 * 2 * 2
        if parts == 2 and devices == blocks == grid and 2 * rows % 128 == 0:
            return fast(series, subject_ids, net_labels, blocks)
        return general(series, subject_ids, net_labels, rows * devices // blocks)

    return jax.shard_map(
        on_device,
        mesh=mesh,
        in_specs=(P(None, None, "blk"), P("parts"), P()),
        out_specs=P(("parts", "blk"), None),
        check_vma=False,
    )
```

```python
import functools

import jax
import jax.numpy as jnp
from jax import lax
from jax.experimental import pallas as pl
from jax.experimental.pallas import tpu as pltpu
from jax.sharding import PartitionSpec as P

CLIP = 0.999
EPS = 1e-05
VMEM = 56 * 2**20


def plans(subjects):
    n = subjects * 5 // 8
    return [(n, subjects - n - 1), (n + 1, subjects - n - 1), (subjects, 0)]


def table_kernel(me_ref, own_ref, other_ref, plan_ref, slots_ref, where_ref, fetch, place):
    subjects = own_ref.shape[0]
    pool = place.shape[1]
    me = me_ref[0]
    one = jnp.int32(1)
    own = jnp.int32(0)
    other = jnp.int32(0)
    for s in range(subjects):
        own = own | (one << own_ref[s])
        other = other | (one << other_ref[s])
    has = (jnp.where(me == 0, own, other), jnp.where(me == 0, other, own))
    both = has[0] & has[1]

    def count(mask):
        total = jnp.int32(0)
        for u in range(pool):
            total = total + ((mask >> u) & 1)
        return total

    distinct = (count(has[0]), count(has[1]))
    common = count(both)
    n = jnp.int32(subjects)
    plan = jnp.int32(0)
    for i, (cand, most) in reversed(list(enumerate(plans(subjects)))):
        short = [jnp.maximum(d - cand, 0) for d in distinct]
        fits = jnp.logical_and(short[0] + short[1] <= common, jnp.maximum(short[0], short[1]) <= most)
        n = jnp.where(fits, cand, n)
        plan = jnp.where(fits, i, plan)
    taken = (jnp.maximum(distinct[0] - n, 0), jnp.maximum(distinct[1] - n, 0))
    plan_ref[0] = plan

    take = [jnp.int32(0), jnp.int32(0)]
    seen = jnp.int32(0)
    for u in range(pool):
        bit = (both >> u) & 1
        first = jnp.where(seen < taken[0], bit, 0)
        second = jnp.where(jnp.logical_and(seen >= taken[0], seen < taken[0] + taken[1]), bit, 0)
        take[0] = take[0] | (first << u)
        take[1] = take[1] | (second << u)
        seen = seen + bit
    for p in range(2):
        for k in range(subjects):
            fetch[p, k] = 0
        ahead = jnp.int32(0)
        behind = taken[1 - p]
        for u in range(pool):
            give = (take[1 - p] >> u) & 1
            keep = (((has[p] & ~take[p]) >> u) & 1) * (1 - give)
            spot = jnp.where(give == 1, ahead, behind)
            place[p, u] = spot

            @pl.when(give + keep == 1)
            def _():
                fetch[p, spot] = u

            ahead = ahead + give
            behind = behind + keep
    mine = jnp.where(me == 0, take[0], take[1])
    for k in range(subjects):
        slots_ref[k] = jnp.where(k < n, fetch[me, k], fetch[1 - me, jnp.maximum(k - n, 0)])
    for s in range(subjects):
        u = own_ref[s]
        from_other = ((mine >> u) & 1) == 1
        where_ref[s] = jnp.where(from_other, n + place[1 - me, u], place[me, u])


def tables(me, own, other, pool):
    subjects = own.shape[0]
    smem = pl.BlockSpec(memory_space=pltpu.SMEM)
    return pl.pallas_call(
        table_kernel,
        in_specs=[smem] * 3,
        out_specs=[smem] * 3,
        out_shape=[
            jax.ShapeDtypeStruct((1,), jnp.int32),
            jax.ShapeDtypeStruct((subjects,), jnp.int32),
            jax.ShapeDtypeStruct((subjects,), jnp.int32),
        ],
        scratch_shapes=[
            pltpu.SMEM((2, subjects), jnp.int32),
            pltpu.SMEM((2, pool), jnp.int32),
        ],
    )(me, own, other)


def normalize_kernel(first, turned, slots_ref, series_ref, out_ref, held, done, sem):
    count = held.shape[0]

    def load(i):
        return pltpu.make_async_copy(series_ref.at[slots_ref[first + i]], held.at[i], sem.at[0, i])

    def store(i):
        return pltpu.make_async_copy(done.at[i], out_ref.at[i], sem.at[1, i])

    for i in range(count):
        load(i).start()

    @pl.loop(0, count)
    def _(i):
        load(i).wait()
        values = held[i].astype(jnp.float32)
        center = values - jnp.mean(values, axis=0, keepdims=True)
        spread = jnp.mean(center * center, axis=0, keepdims=True)
        value = center * (1 / jnp.sqrt(spread + EPS))
        done[i] = (value.T if turned else value).astype(jnp.bfloat16)
        store(i).start()

    for i in range(count):
        store(i).wait()


def normalize_slots(series, slots, first, last, turned=False):
    _, frames, rows = series.shape
    shape = (rows, frames) if turned else (frames, rows)
    count = last - first
    any_spec = pl.BlockSpec(memory_space=pl.ANY)
    return pl.pallas_call(
        functools.partial(normalize_kernel, first, turned),
        in_specs=[pl.BlockSpec(memory_space=pltpu.SMEM), any_spec],
        out_specs=any_spec,
        out_shape=jax.ShapeDtypeStruct((count, *shape), jnp.bfloat16),
        scratch_shapes=[
            pltpu.VMEM((count, frames, rows), jnp.bfloat16),
            pltpu.VMEM((count, *shape), jnp.bfloat16),
            pltpu.SemaphoreType.DMA((2, count)),
        ],
        compiler_params=pltpu.CompilerParams(vmem_limit_bytes=VMEM),
        cost_estimate=pl.CostEstimate(
            flops=8 * count * frames * rows,
            bytes_accessed=4 * count * frames * rows,
            transcendentals=0,
        ),
    )(slots, series)


def fisher_kernel(codes, blanks, entries, arrays, has_prev, step, *refs):
    me_ref, labels_ref, where_ref, left_hbm = refs[:4]
    sources = refs[4 : 4 + arrays]
    out_ref, left_ref, buffer, half_ref, tile, blank, todo, left_sem, fetch_sem, tile_sem, blank_sem = refs[
        4 + arrays + has_prev :
    ]
    count = len(codes)
    _, rows, frames = left_ref.shape
    width = buffer.shape[3]
    subjects = where_ref.shape[0]
    me = me_ref[0]
    core = me & 1
    label = labels_ref[me]
    scale = jnp.float32(frames)
    limit = jnp.float32(CLIP * frames)

    def pair_of(code):
        return (me >> 1) ^ code

    def columns(pair):
        return out_ref.at[:, pl.ds(pl.multiple_of(pair * (2 * width), 128), 2 * width)]

    total = jnp.int32(0)
    for j, code in enumerate(codes):
        for h in range(2):
            todo[total] = 2 * j + h
            total = total + jnp.where(labels_ref[2 * pair_of(code) + h] == label, 1, 0)

    def start_fetch(i, slot):
        item = todo[i]
        entry = (item & ~1) | jnp.where((item & 1) == core, 0, 1)
        for e, pieces in enumerate(entries):

            @pl.when(entry == e)
            def _():
                at = 0
                for array, first, span in pieces:
                    pltpu.make_async_copy(
                        sources[array].at[pl.ds(first, span)], buffer.at[slot, pl.ds(at, span)], fetch_sem.at[slot]
                    ).start()
                    at += span

    left_copy = pltpu.make_async_copy(left_hbm, left_ref, left_sem.at[0])

    @pl.when(total > 0)
    def _():
        left_copy.start()
        start_fetch(0, 0)

    if blanks:
        blank[...] = jnp.zeros_like(blank)
    empty = []
    for j, code in enumerate(blanks):
        pair = pair_of(code)
        unwanted = jnp.logical_and(labels_ref[2 * pair] != label, labels_ref[2 * pair + 1] != label)
        empty.append((unwanted, pltpu.make_async_copy(blank, columns(pair), blank_sem.at[j])))

        @pl.when(unwanted)
        def _(j=j):
            empty[j][1].start()

    def tile_copy(pair, slot):
        return pltpu.make_async_copy(tile.at[slot], columns(pair), tile_sem.at[slot])

    def code_of(j):
        code = jnp.int32(codes[0])
        for k in range(1, count):
            code = jnp.where(j == k, codes[k], code)
        return code

    chunk = min(256, width)

    @pl.when(total > 0)
    def _():
        left_copy.wait()

    def body(i, pairs):
        slot = i % 2
        item = todo[i]
        j = item >> 1
        h = item & 1
        opens = jnp.logical_or(i == 0, (todo[jnp.maximum(i - 1, 0)] >> 1) != j)
        closes = jnp.logical_or(i == total - 1, (todo[jnp.minimum(i + 1, total - 1)] >> 1) != j)
        pairs = pairs + jnp.where(opens, 1, 0)
        spot = pairs % 2

        @pl.when(i + 1 < total)
        def _():
            start_fetch(i + 1, 1 - slot)

        @pl.when(jnp.logical_and(opens, pairs > 2))
        def _():
            tile_copy(0, spot).wait()

        @pl.when(jnp.logical_and(opens, closes))
        def _():
            tile[spot] = jnp.zeros(tile.shape[1:], jnp.float32)

        pltpu.make_async_copy(buffer.at[slot], buffer.at[slot], fetch_sem.at[slot]).wait()

        @pl.loop(0, rows // step)
        def _(r):
            band = pl.ds(pl.multiple_of(r * step, 16), step)
            for low in range(0, width, chunk):
                high = min(low + chunk, width)
                up = down = None
                for s in range(subjects):
                    k = where_ref[s]
                    corr = jnp.dot(
                        left_ref[k, band, :], buffer[slot, k, :, low:high], preferred_element_type=jnp.float32
                    )
                    corr = jnp.clip(corr, -limit, limit)
                    plus, minus = scale + corr, scale - corr
                    up = plus if up is None else up * plus
                    down = minus if down is None else down * minus
                half_ref[band, low:high] = 0.5 * jnp.log(up / down)

        for half in range(2):

            @pl.when(h == half)
            def _():
                tile[spot, :, half * width : (half + 1) * width] = half_ref[...]

        @pl.when(closes)
        def _():
            tile_copy(pair_of(code_of(j)), spot).start()

        return pairs

    pairs = lax.fori_loop(0, total, body, jnp.int32(0))

    @pl.when(pairs > 0)
    def _():
        tile_copy(0, pairs % 2).wait()

    @pl.when(pairs > 1)
    def _():
        tile_copy(0, (pairs + 1) % 2).wait()

    for unwanted, copy in empty:

        @pl.when(unwanted)
        def _():
            copy.wait()


def band_rows(rows):
    return next(k for k in range(min(rows, 192), 0, -1) if rows % k == 0 and (k % 16 == 0 or k == rows))


def fisher(me, labels, where, left, pairs, blanks=(), prev=None):
    slots, rows, frames = left.shape
    width = rows
    any_spec = pl.BlockSpec(memory_space=pl.ANY)
    smem = pl.BlockSpec(memory_space=pltpu.SMEM)
    arrays, entries = [], []
    for _, *sides in pairs:
        for side in sides:
            entry = []
            for array, first, span in side:
                known = [k for k, x in enumerate(arrays) if x is array]
                if not known:
                    arrays.append(array)
                    known = [len(arrays) - 1]
                entry.append((known[0], first, span))
            entries.append(entry)
    operands = [me, labels, where, left, *arrays] + ([] if prev is None else [prev])
    codes = [pair[0] for pair in pairs]
    return pl.pallas_call(
        functools.partial(
            fisher_kernel, codes, blanks, entries, len(arrays), int(prev is not None), band_rows(rows)
        ),
        in_specs=[smem] * 3 + [any_spec] * (len(operands) - 3),
        out_specs=any_spec,
        out_shape=jax.ShapeDtypeStruct((rows, labels.shape[0] * width), jnp.float32),
        scratch_shapes=[
            pltpu.VMEM((slots, rows, frames), jnp.bfloat16),
            pltpu.VMEM((2, slots, frames, width), jnp.bfloat16),
            pltpu.VMEM((rows, width), jnp.float32),
            pltpu.VMEM((2, rows, 2 * width), jnp.float32),
            pltpu.VMEM((rows, 2 * width), jnp.float32),
            pltpu.SMEM((2 * len(codes) + 1,), jnp.int32),
            pltpu.SemaphoreType.DMA((1,)),
            pltpu.SemaphoreType.DMA((2,)),
            pltpu.SemaphoreType.DMA((2,)),
            pltpu.SemaphoreType.DMA((max(len(blanks), 1),)),
        ],
        input_output_aliases={} if prev is None else {len(operands) - 1: 0},
        compiler_params=pltpu.CompilerParams(vmem_limit_bytes=VMEM),
        cost_estimate=pl.CostEstimate(
            flops=2 * rows * width * frames * slots * len(codes),
            bytes_accessed=rows * width * 8 * max(len(codes), len(blanks)),
            transcendentals=rows * width * len(codes),
        ),
    )(*operands)


def pack_kernel(spans, *refs):
    sources, out_ref, held, sem = refs[: len(spans)], refs[-3], refs[-2], refs[-1]
    loads, stores, at = [], [], 0
    for k, span in enumerate(spans):
        place = pl.ds(at, span)
        loads.append(pltpu.make_async_copy(sources[k], held.at[place], sem.at[0, k]))
        stores.append(pltpu.make_async_copy(held.at[place], out_ref.at[place], sem.at[1, k]))
        at += span
    for copy in loads:
        copy.start()
    for load, store in zip(loads, stores):
        load.wait()
        store.start()
    for copy in stores:
        copy.wait()


def pack(*arrays):
    spans = [x.shape[0] for x in arrays]
    shape = (sum(spans), *arrays[0].shape[1:])
    size = 2 * shape[0] * shape[1] * shape[2]
    any_spec = pl.BlockSpec(memory_space=pl.ANY)
    return pl.pallas_call(
        functools.partial(pack_kernel, spans),
        in_specs=[any_spec] * len(spans),
        out_specs=any_spec,
        out_shape=jax.ShapeDtypeStruct(shape, arrays[0].dtype),
        scratch_shapes=[pltpu.VMEM(shape, arrays[0].dtype), pltpu.SemaphoreType.DMA((2, len(spans)))],
        compiler_params=pltpu.CompilerParams(vmem_limit_bytes=VMEM),
        cost_estimate=pl.CostEstimate(flops=0, bytes_accessed=2 * size, transcendentals=0),
    )(*arrays)


def fast(series, subject_ids, net_labels, blocks):
    pool = series.shape[0]
    subjects = subject_ids.shape[0]
    index = lax.axis_index("blk").astype(jnp.int32)
    part = lax.axis_index("parts").astype(jnp.int32)
    other = lax.ppermute(subject_ids, "parts", [(0, 1), (1, 0)])
    plan, slots, where = tables(part[None], subject_ids, other, pool)

    last = (blocks - 1) >> 2
    inner = [i for i in range(blocks) if 0 < i >> 2 < last]
    at_end = jnp.logical_or(index >> 2 == 0, index >> 2 == last)

    def sender(perm):
        return lambda x: lax.ppermute(x, "blk", perm)

    core = sender([(i, i ^ 1) for i in range(blocks)])
    along_x = sender([(i, i ^ 2) for i in range(blocks)])
    along_z = sender([(i, i ^ 4) for i in range(blocks)])
    middle = sender([(i, i ^ 12) for i in inner])
    outward = sender([(i, i ^ 4) for i in inner])

    def branch(n, m):
        half = (n + 1) // 2
        together = lax.optimization_barrier

        def along_y(*arrays):
            if not m:
                return None
            return lax.ppermute(jnp.concatenate([x[:m] for x in arrays]), "parts", [(0, 1), (1, 0)])

        def twin(x):
            return None if x is None else core(x)

        def fit(*pieces):
            return [p for p in pieces if p[2]]

        def run(series, slots, where, net_labels):
            step = functools.partial(fisher, index[None], net_labels, where)

            def pair(code, a, y, k, both, y_s):
                return code, fit((a, 0, n), (y, k * m, m)), fit((both, k * n, n), (y_s, k * m, m))

            own = normalize_slots(series, slots, 0, n)
            r1, mid, x0, own_s = along_z(own), middle(own), along_x(own), core(own)
            taken = normalize_slots(series, slots, n, n + m) if m else None
            taken_s = twin(taken)
            left = normalize_slots(series, slots, 0, n + m, turned=True)
            r1, mid, x0, own_s, taken, taken_s, left = together((r1, mid, x0, own_s, taken, taken_s, left))

            e2, b2, x1, y1 = outward(mid), middle(r1), along_x(r1), along_y(r1, x0)
            joint2 = pack(r1, x0)
            out = step(
                left,
                [(0, fit((own, 0, n), (taken, 0, m)), fit((own_s, 0, n), (taken_s, 0, m)))],
                blanks=tuple(range(blocks // 2)),
            )
            r2 = jnp.where(at_end, e2, b2)
            r2, x1, y1, joint2, out = together((r2, x1, y1, joint2, out))

            r3, x2, y2, core2, y1_s = along_z(r2), along_x(r2), along_y(r2, x1), core(joint2), twin(y1)
            joint3 = pack(r2, x1)
            r3, x2, y2, core2, y1_s, joint3 = together((r3, x2, y2, core2, y1_s, joint3))

            x3, rest, y3 = along_x(r3[:half]), along_z(x2[half:]), along_y(r3, x2)
            core3, y2_s = core(joint3), twin(y2)
            joint4 = pack(r3, x2)
            out = step(
                left,
                [pair(2, r1, y1, 0, core2, y1_s), pair(1, x0, y1, 1, core2, y1_s)],
                prev=out,
            )
            rest, x3, y3, core3, y2_s, joint4, out = together((rest, x3, y3, core3, y2_s, joint4, out))

            y4, core4, y3_s, x3_s, rest_s = along_y(x3), core(joint4), twin(y3), core(x3), core(rest)
            out = step(
                left,
                [pair(4, r2, y2, 0, core3, y2_s), pair(3, x1, y2, 1, core3, y2_s)],
                prev=out,
            )
            y4, core4, y3_s, x3_s, rest_s, out = together((y4, core4, y3_s, x3_s, rest_s, out))

            y4_s = twin(y4)
            mine = fit((x3, 0, half), (rest, 0, n - half), (y4, 0, m))
            sibling = fit((x3_s, 0, half), (rest_s, 0, n - half), (y4_s, 0, m))
            return step(
                left,
                [
                    pair(6, r3, y3, 0, core4, y3_s),
                    pair(5, x2, y3, 1, core4, y3_s),
                    (7, mine, sibling),
                ],
                prev=out,
            )

        return run

    def unshared(series, slots, where, net_labels):
        own = normalize_slots(series, slots, 0, subjects)
        left = normalize_slots(series, slots, 0, subjects, turned=True)
        r1 = along_z(own)
        r2 = jnp.where(at_end, outward(middle(own)), middle(r1))
        column = [own, r1, r2, along_z(r2)]
        mine = column + [along_x(x) for x in column]
        codes = [0, 2, 4, 6, 1, 3, 5, 7]

        def whole(x):
            return [(x, 0, subjects)]

        pairs = [(code, whole(x), whole(core(x))) for code, x in zip(codes, mine)]
        return fisher(index[None], net_labels, where, left, pairs, blanks=tuple(range(blocks // 2)))

    runs = [branch(n, m) if m else unshared for n, m in plans(subjects)]
    return lax.switch(plan[0], runs, series, slots, where, net_labels)


def general(series, subject_ids, net_labels, block):
    chosen = jnp.take(series, subject_ids, axis=0).astype(jnp.float32)
    center = chosen - jnp.mean(chosen, axis=1, keepdims=True)
    spread = jnp.mean(center * center, axis=1, keepdims=True)
    left = (center / jnp.sqrt(spread + EPS)).astype(jnp.bfloat16)
    subjects, frames, rows = left.shape
    right = lax.all_gather(left, "blk", axis=2, tiled=True)
    row_labels = jnp.repeat(net_labels, block)
    own_labels = lax.dynamic_slice_in_dim(row_labels, lax.axis_index("blk") * rows, rows)
    up = down = jnp.float32(1)
    for s in range(subjects):
        corr = lax.dot_general(
            left[s], right[s], (((0,), (0,)), ((), ())), preferred_element_type=jnp.float32
        )
        corr = jnp.clip(corr / frames, -CLIP, CLIP)
        up, down = up * (1 + corr), down * (1 - corr)
    total = 0.5 * jnp.log(up / down)
    return jnp.where(own_labels[:, None] == row_labels[None, :], total, jnp.zeros_like(total))


def solution(mesh):
    parts, devices = mesh.shape["parts"], mesh.shape["blk"]

    def on_device(series, subject_ids, net_labels):
        blocks = net_labels.shape[0]
        rows = series.shape[2]
        grid = 4 * 2 * 2
        if parts == 2 and devices == blocks == grid and 2 * rows % 128 == 0:
            return fast(series, subject_ids, net_labels, blocks)
        return general(series, subject_ids, net_labels, rows * devices // blocks)

    return jax.shard_map(
        on_device,
        mesh=mesh,
        in_specs=(P(None, None, "blk"), P("parts"), P()),
        out_specs=P(("parts", "blk"), None),
        check_vma=False,
    )
```

```python
import functools

import jax
import jax.numpy as jnp
from jax import lax
from jax.experimental import pallas as pl
from jax.experimental.pallas import tpu as pltpu
from jax.sharding import PartitionSpec as P

CLIP = 0.999
EPS = 1e-05
VMEM = 56 * 2**20


def plans(subjects):
    n = subjects * 5 // 8
    return [(n, subjects - n - 1), (n + 1, subjects - n - 1), (subjects, 0)]


def table_kernel(me_ref, own_ref, other_ref, plan_ref, slots_ref, where_ref, fetch, place):
    subjects = own_ref.shape[0]
    pool = place.shape[1]
    me = me_ref[0]
    one = jnp.int32(1)
    own = jnp.int32(0)
    other = jnp.int32(0)
    for s in range(subjects):
        own = own | (one << own_ref[s])
        other = other | (one << other_ref[s])
    has = (jnp.where(me == 0, own, other), jnp.where(me == 0, other, own))
    both = has[0] & has[1]

    def count(mask):
        total = jnp.int32(0)
        for u in range(pool):
            total = total + ((mask >> u) & 1)
        return total

    distinct = (count(has[0]), count(has[1]))
    common = count(both)
    n = jnp.int32(subjects)
    plan = jnp.int32(0)
    for i, (cand, most) in reversed(list(enumerate(plans(subjects)))):
        short = [jnp.maximum(d - cand, 0) for d in distinct]
        fits = jnp.logical_and(short[0] + short[1] <= common, jnp.maximum(short[0], short[1]) <= most)
        n = jnp.where(fits, cand, n)
        plan = jnp.where(fits, i, plan)
    taken = (jnp.maximum(distinct[0] - n, 0), jnp.maximum(distinct[1] - n, 0))
    plan_ref[0] = plan

    take = [jnp.int32(0), jnp.int32(0)]
    seen = jnp.int32(0)
    for u in range(pool):
        bit = (both >> u) & 1
        first = jnp.where(seen < taken[0], bit, 0)
        second = jnp.where(jnp.logical_and(seen >= taken[0], seen < taken[0] + taken[1]), bit, 0)
        take[0] = take[0] | (first << u)
        take[1] = take[1] | (second << u)
        seen = seen + bit
    for p in range(2):
        for k in range(subjects):
            fetch[p, k] = 0
        ahead = jnp.int32(0)
        behind = taken[1 - p]
        for u in range(pool):
            give = (take[1 - p] >> u) & 1
            keep = (((has[p] & ~take[p]) >> u) & 1) * (1 - give)
            spot = jnp.where(give == 1, ahead, behind)
            place[p, u] = spot

            @pl.when(give + keep == 1)
            def _():
                fetch[p, spot] = u

            ahead = ahead + give
            behind = behind + keep
    mine = jnp.where(me == 0, take[0], take[1])
    for k in range(subjects):
        slots_ref[k] = jnp.where(k < n, fetch[me, k], fetch[1 - me, jnp.maximum(k - n, 0)])
    for s in range(subjects):
        u = own_ref[s]
        from_other = ((mine >> u) & 1) == 1
        where_ref[s] = jnp.where(from_other, n + place[1 - me, u], place[me, u])


def tables(me, own, other, pool):
    subjects = own.shape[0]
    smem = pl.BlockSpec(memory_space=pltpu.SMEM)
    return pl.pallas_call(
        table_kernel,
        in_specs=[smem] * 3,
        out_specs=[smem] * 3,
        out_shape=[
            jax.ShapeDtypeStruct((1,), jnp.int32),
            jax.ShapeDtypeStruct((subjects,), jnp.int32),
            jax.ShapeDtypeStruct((subjects,), jnp.int32),
        ],
        scratch_shapes=[
            pltpu.SMEM((2, subjects), jnp.int32),
            pltpu.SMEM((2, pool), jnp.int32),
        ],
    )(me, own, other)


def normalize_kernel(first, turned, slots_ref, series_ref, out_ref, held, done, sem):
    count = held.shape[0]

    def load(i):
        return pltpu.make_async_copy(series_ref.at[slots_ref[first + i]], held.at[i], sem.at[0, i])

    def store(i):
        return pltpu.make_async_copy(done.at[i], out_ref.at[i], sem.at[1, i])

    for i in range(count):
        load(i).start()

    @pl.loop(0, count)
    def _(i):
        load(i).wait()
        values = held[i].astype(jnp.float32)
        center = values - jnp.mean(values, axis=0, keepdims=True)
        spread = jnp.mean(center * center, axis=0, keepdims=True)
        value = center * (1 / jnp.sqrt(spread + EPS))
        done[i] = (value.T if turned else value).astype(jnp.bfloat16)
        store(i).start()

    for i in range(count):
        store(i).wait()


def normalize_slots(series, slots, first, last, turned=False):
    _, frames, rows = series.shape
    shape = (rows, frames) if turned else (frames, rows)
    count = last - first
    any_spec = pl.BlockSpec(memory_space=pl.ANY)
    return pl.pallas_call(
        functools.partial(normalize_kernel, first, turned),
        in_specs=[pl.BlockSpec(memory_space=pltpu.SMEM), any_spec],
        out_specs=any_spec,
        out_shape=jax.ShapeDtypeStruct((count, *shape), jnp.bfloat16),
        scratch_shapes=[
            pltpu.VMEM((count, frames, rows), jnp.bfloat16),
            pltpu.VMEM((count, *shape), jnp.bfloat16),
            pltpu.SemaphoreType.DMA((2, count)),
        ],
        compiler_params=pltpu.CompilerParams(vmem_limit_bytes=VMEM),
        cost_estimate=pl.CostEstimate(
            flops=8 * count * frames * rows,
            bytes_accessed=4 * count * frames * rows,
            transcendentals=0,
        ),
    )(slots, series)


def fisher_kernel(codes, blanks, entries, arrays, has_prev, step, *refs):
    me_ref, labels_ref, where_ref, left_hbm = refs[:4]
    sources = refs[4 : 4 + arrays]
    out_ref, left_ref, buffer, half_ref, tile, blank, todo, left_sem, fetch_sem, tile_sem, blank_sem = refs[
        4 + arrays + has_prev :
    ]
    count = len(codes)
    _, rows, frames = left_ref.shape
    width = buffer.shape[3]
    subjects = where_ref.shape[0]
    me = me_ref[0]
    core = me & 1
    label = labels_ref[me]
    scale = jnp.float32(frames)
    limit = jnp.float32(CLIP * frames)

    def pair_of(code):
        return (me >> 1) ^ code

    def columns(pair):
        return out_ref.at[:, pl.ds(pl.multiple_of(pair * (2 * width), 128), 2 * width)]

    total = jnp.int32(0)
    for j, code in enumerate(codes):
        for h in range(2):
            todo[total] = 2 * j + h
            total = total + jnp.where(labels_ref[2 * pair_of(code) + h] == label, 1, 0)

    def start_fetch(i, slot):
        item = todo[i]
        entry = (item & ~1) | jnp.where((item & 1) == core, 0, 1)
        for e, pieces in enumerate(entries):

            @pl.when(entry == e)
            def _():
                at = 0
                for array, first, span in pieces:
                    pltpu.make_async_copy(
                        sources[array].at[pl.ds(first, span)], buffer.at[slot, pl.ds(at, span)], fetch_sem.at[slot]
                    ).start()
                    at += span

    left_copy = pltpu.make_async_copy(left_hbm, left_ref, left_sem.at[0])

    @pl.when(total > 0)
    def _():
        left_copy.start()
        start_fetch(0, 0)

    if blanks:
        blank[...] = jnp.zeros_like(blank)
    empty = []
    for j, code in enumerate(blanks):
        pair = pair_of(code)
        unwanted = jnp.logical_and(labels_ref[2 * pair] != label, labels_ref[2 * pair + 1] != label)
        empty.append((unwanted, pltpu.make_async_copy(blank, columns(pair), blank_sem.at[j])))

        @pl.when(unwanted)
        def _(j=j):
            empty[j][1].start()

    def tile_copy(pair, slot):
        return pltpu.make_async_copy(tile.at[slot], columns(pair), tile_sem.at[slot])

    def code_of(j):
        code = jnp.int32(codes[0])
        for k in range(1, count):
            code = jnp.where(j == k, codes[k], code)
        return code

    chunk = min(256, width)

    @pl.when(total > 0)
    def _():
        left_copy.wait()

    def body(i, pairs):
        slot = i % 2
        item = todo[i]
        j = item >> 1
        h = item & 1
        opens = jnp.logical_or(i == 0, (todo[jnp.maximum(i - 1, 0)] >> 1) != j)
        closes = jnp.logical_or(i == total - 1, (todo[jnp.minimum(i + 1, total - 1)] >> 1) != j)
        pairs = pairs + jnp.where(opens, 1, 0)
        spot = pairs % 2

        @pl.when(i + 1 < total)
        def _():
            start_fetch(i + 1, 1 - slot)

        @pl.when(jnp.logical_and(opens, pairs > 2))
        def _():
            tile_copy(0, spot).wait()

        @pl.when(jnp.logical_and(opens, closes))
        def _():
            tile[spot] = jnp.zeros(tile.shape[1:], jnp.float32)

        pltpu.make_async_copy(buffer.at[slot], buffer.at[slot], fetch_sem.at[slot]).wait()

        @pl.loop(0, rows // step)
        def _(r):
            band = pl.ds(pl.multiple_of(r * step, 16), step)
            for low in range(0, width, chunk):
                high = min(low + chunk, width)
                up = down = None
                for s in range(subjects):
                    k = where_ref[s]
                    corr = jnp.dot(
                        left_ref[k, band, :], buffer[slot, k, :, low:high], preferred_element_type=jnp.float32
                    )
                    corr = jnp.clip(corr, -limit, limit)
                    plus, minus = scale + corr, scale - corr
                    up = plus if up is None else up * plus
                    down = minus if down is None else down * minus
                half_ref[band, low:high] = 0.5 * jnp.log(up / down)

        for half in range(2):

            @pl.when(h == half)
            def _():
                tile[spot, :, half * width : (half + 1) * width] = half_ref[...]

        @pl.when(closes)
        def _():
            tile_copy(pair_of(code_of(j)), spot).start()

        return pairs

    pairs = lax.fori_loop(0, total, body, jnp.int32(0))

    @pl.when(pairs > 0)
    def _():
        tile_copy(0, pairs % 2).wait()

    @pl.when(pairs > 1)
    def _():
        tile_copy(0, (pairs + 1) % 2).wait()

    for unwanted, copy in empty:

        @pl.when(unwanted)
        def _():
            copy.wait()


def band_rows(rows, longest):
    return next(k for k in range(min(rows, longest), 0, -1) if rows % k == 0 and (k % 16 == 0 or k == rows))


def fisher(me, labels, where, left, pairs, blanks=(), prev=None, longest=192):
    slots, rows, frames = left.shape
    width = rows
    any_spec = pl.BlockSpec(memory_space=pl.ANY)
    smem = pl.BlockSpec(memory_space=pltpu.SMEM)
    arrays, entries = [], []
    for _, *sides in pairs:
        for side in sides:
            entry = []
            for array, first, span in side:
                known = [k for k, x in enumerate(arrays) if x is array]
                if not known:
                    arrays.append(array)
                    known = [len(arrays) - 1]
                entry.append((known[0], first, span))
            entries.append(entry)
    operands = [me, labels, where, left, *arrays] + ([] if prev is None else [prev])
    codes = [pair[0] for pair in pairs]
    return pl.pallas_call(
        functools.partial(
            fisher_kernel, codes, blanks, entries, len(arrays), int(prev is not None), band_rows(rows, longest)
        ),
        in_specs=[smem] * 3 + [any_spec] * (len(operands) - 3),
        out_specs=any_spec,
        out_shape=jax.ShapeDtypeStruct((rows, labels.shape[0] * width), jnp.float32),
        scratch_shapes=[
            pltpu.VMEM((slots, rows, frames), jnp.bfloat16),
            pltpu.VMEM((2, slots, frames, width), jnp.bfloat16),
            pltpu.VMEM((rows, width), jnp.float32),
            pltpu.VMEM((2, rows, 2 * width), jnp.float32),
            pltpu.VMEM((rows, 2 * width), jnp.float32),
            pltpu.SMEM((2 * len(codes) + 1,), jnp.int32),
            pltpu.SemaphoreType.DMA((1,)),
            pltpu.SemaphoreType.DMA((2,)),
            pltpu.SemaphoreType.DMA((2,)),
            pltpu.SemaphoreType.DMA((max(len(blanks), 1),)),
        ],
        input_output_aliases={} if prev is None else {len(operands) - 1: 0},
        compiler_params=pltpu.CompilerParams(vmem_limit_bytes=VMEM),
        cost_estimate=pl.CostEstimate(
            flops=2 * rows * width * frames * slots * len(codes),
            bytes_accessed=rows * width * 8 * max(len(codes), len(blanks)),
            transcendentals=rows * width * len(codes),
        ),
    )(*operands)


def pack_kernel(spans, *refs):
    sources, out_ref, held, sem = refs[: len(spans)], refs[-3], refs[-2], refs[-1]
    loads, stores, at = [], [], 0
    for k, span in enumerate(spans):
        place = pl.ds(at, span)
        loads.append(pltpu.make_async_copy(sources[k], held.at[place], sem.at[0, k]))
        stores.append(pltpu.make_async_copy(held.at[place], out_ref.at[place], sem.at[1, k]))
        at += span
    for copy in loads:
        copy.start()
    for load, store in zip(loads, stores):
        load.wait()
        store.start()
    for copy in stores:
        copy.wait()


def pack(*arrays):
    spans = [x.shape[0] for x in arrays]
    shape = (sum(spans), *arrays[0].shape[1:])
    size = 2 * shape[0] * shape[1] * shape[2]
    any_spec = pl.BlockSpec(memory_space=pl.ANY)
    return pl.pallas_call(
        functools.partial(pack_kernel, spans),
        in_specs=[any_spec] * len(spans),
        out_specs=any_spec,
        out_shape=jax.ShapeDtypeStruct(shape, arrays[0].dtype),
        scratch_shapes=[pltpu.VMEM(shape, arrays[0].dtype), pltpu.SemaphoreType.DMA((2, len(spans)))],
        compiler_params=pltpu.CompilerParams(vmem_limit_bytes=VMEM),
        cost_estimate=pl.CostEstimate(flops=0, bytes_accessed=2 * size, transcendentals=0),
    )(*arrays)


def fast(series, subject_ids, net_labels, blocks):
    pool = series.shape[0]
    subjects = subject_ids.shape[0]
    index = lax.axis_index("blk").astype(jnp.int32)
    part = lax.axis_index("parts").astype(jnp.int32)
    other = lax.ppermute(subject_ids, "parts", [(0, 1), (1, 0)])
    plan, slots, where = tables(part[None], subject_ids, other, pool)

    last = (blocks - 1) >> 2
    inner = [i for i in range(blocks) if 0 < i >> 2 < last]
    at_end = jnp.logical_or(index >> 2 == 0, index >> 2 == last)

    def sender(perm):
        return lambda x: lax.ppermute(x, "blk", perm)

    core = sender([(i, i ^ 1) for i in range(blocks)])
    along_x = sender([(i, i ^ 2) for i in range(blocks)])
    along_z = sender([(i, i ^ 4) for i in range(blocks)])
    middle = sender([(i, i ^ 12) for i in inner])
    outward = sender([(i, i ^ 4) for i in inner])

    def branch(n, m):
        half = m
        together = lax.optimization_barrier

        def along_y(*arrays):
            if not m:
                return None
            joint = jnp.concatenate([x[:m] for x in arrays]) if len(arrays) > 1 else arrays[0][:m]
            return lax.ppermute(joint, "parts", [(0, 1), (1, 0)])

        def twin(x):
            return None if x is None else core(x)

        def fit(*pieces):
            return [p for p in pieces if p[2]]

        def run(series, slots, where, net_labels):
            step = functools.partial(fisher, index[None], net_labels, where)

            def pair(code, a, y, k, both, y_s):
                return code, fit((a, 0, n), (y, k * m, m)), fit((both, k * n, n), (y_s, k * m, m))

            own = normalize_slots(series, slots, 0, n)
            r1, mid, x0, own_s = along_z(own), middle(own), along_x(own), core(own)
            taken = normalize_slots(series, slots, n, n + m) if m else None
            taken_s = twin(taken)
            left = normalize_slots(series, slots, 0, n + m, turned=True)
            r1, mid, x0, own_s, taken, taken_s, left = together((r1, mid, x0, own_s, taken, taken_s, left))

            e2, b2, x1, y1 = outward(mid), middle(r1), along_x(r1), along_y(r1, x0)
            joint2 = pack(r1, x0)
            out = step(
                left,
                [(0, fit((own, 0, n), (taken, 0, m)), fit((own_s, 0, n), (taken_s, 0, m)))],
                blanks=tuple(range(blocks // 2)),
                longest=64,
            )
            r2 = jnp.where(at_end, e2, b2)
            r2, x1, y1, joint2, out = together((r2, x1, y1, joint2, out))

            r3, x2, y2, core2, y1_s = along_z(r2), along_x(r2), along_y(r2, x1), core(joint2), twin(y1)
            joint3 = pack(r2, x1)
            r3, x2, y2, core2, y1_s, joint3 = together((r3, x2, y2, core2, y1_s, joint3))

            x3, rest, y3 = along_x(r3[:half]), along_z(x2[half:]), along_y(r3, x2)
            core3, y2_s = core(joint3), twin(y2)
            joint4 = pack(r3, x2)
            out = step(
                left,
                [pair(2, r1, y1, 0, core2, y1_s), pair(1, x0, y1, 1, core2, y1_s)],
                prev=out,
                longest=64,
            )
            rest, x3, y3, core3, y2_s, joint4, out = together((rest, x3, y3, core3, y2_s, joint4, out))

            y4, core4, y3_s, x3_s, rest_s = along_y(x3), core(joint4), twin(y3), core(x3), core(rest)
            out = step(
                left,
                [pair(4, r2, y2, 0, core3, y2_s), pair(3, x1, y2, 1, core3, y2_s)],
                prev=out,
            )
            y4, core4, y3_s, x3_s, rest_s, out = together((y4, core4, y3_s, x3_s, rest_s, out))

            y4_s = twin(y4)
            mine = fit((x3, 0, half), (rest, 0, n - half), (y4, 0, m))
            sibling = fit((x3_s, 0, half), (rest_s, 0, n - half), (y4_s, 0, m))
            return step(
                left,
                [
                    pair(6, r3, y3, 0, core4, y3_s),
                    pair(5, x2, y3, 1, core4, y3_s),
                    (7, mine, sibling),
                ],
                prev=out,
                longest=384,
            )

        return run

    def unshared(series, slots, where, net_labels):
        own = normalize_slots(series, slots, 0, subjects)
        left = normalize_slots(series, slots, 0, subjects, turned=True)
        r1 = along_z(own)
        r2 = jnp.where(at_end, outward(middle(own)), middle(r1))
        column = [own, r1, r2, along_z(r2)]
        mine = column + [along_x(x) for x in column]
        codes = [0, 2, 4, 6, 1, 3, 5, 7]

        def whole(x):
            return [(x, 0, subjects)]

        pairs = [(code, whole(x), whole(core(x))) for code, x in zip(codes, mine)]
        return fisher(
            index[None], net_labels, where, left, pairs, blanks=tuple(range(blocks // 2)), longest=64
        )

    runs = [branch(n, m) if m else unshared for n, m in plans(subjects)]
    return lax.switch(plan[0], runs, series, slots, where, net_labels)


def general(series, subject_ids, net_labels, block):
    chosen = jnp.take(series, subject_ids, axis=0).astype(jnp.float32)
    center = chosen - jnp.mean(chosen, axis=1, keepdims=True)
    spread = jnp.mean(center * center, axis=1, keepdims=True)
    left = (center / jnp.sqrt(spread + EPS)).astype(jnp.bfloat16)
    subjects, frames, rows = left.shape
    right = lax.all_gather(left, "blk", axis=2, tiled=True)
    row_labels = jnp.repeat(net_labels, block)
    own_labels = lax.dynamic_slice_in_dim(row_labels, lax.axis_index("blk") * rows, rows)
    up = down = jnp.float32(1)
    for s in range(subjects):
        corr = lax.dot_general(
            left[s], right[s], (((0,), (0,)), ((), ())), preferred_element_type=jnp.float32
        )
        corr = jnp.clip(corr / frames, -CLIP, CLIP)
        up, down = up * (1 + corr), down * (1 - corr)
    total = 0.5 * jnp.log(up / down)
    return jnp.where(own_labels[:, None] == row_labels[None, :], total, jnp.zeros_like(total))


def solution(mesh):
    parts, devices = mesh.shape["parts"], mesh.shape["blk"]

    def on_device(series, subject_ids, net_labels):
        blocks = net_labels.shape[0]
        rows = series.shape[2]
        grid = 4 * 2 * 2
        if parts == 2 and devices == blocks == grid and 2 * rows % 128 == 0:
            return fast(series, subject_ids, net_labels, blocks)
        return general(series, subject_ids, net_labels, rows * devices // blocks)

    return jax.shard_map(
        on_device,
        mesh=mesh,
        in_specs=(P(None, None, "blk"), P("parts"), P()),
        out_specs=P(("parts", "blk"), None),
        check_vma=False,
    )
```

```python
import functools

import jax
import jax.numpy as jnp
from jax import lax
from jax.experimental import pallas as pl
from jax.experimental.pallas import tpu as pltpu
from jax.sharding import PartitionSpec as P

CLIP = 0.999
EPS = 1e-05
VMEM = 56 * 2**20


def plans(subjects):
    n = subjects * 5 // 8
    return [(n, subjects - n - 1), (n + 1, subjects - n - 1), (subjects, 0)]


def table_kernel(me_ref, own_ref, other_ref, plan_ref, slots_ref, where_ref, fetch, place):
    subjects = own_ref.shape[0]
    pool = place.shape[1]
    me = me_ref[0]
    one = jnp.int32(1)
    own = jnp.int32(0)
    other = jnp.int32(0)
    for s in range(subjects):
        own = own | (one << own_ref[s])
        other = other | (one << other_ref[s])
    has = (jnp.where(me == 0, own, other), jnp.where(me == 0, other, own))
    both = has[0] & has[1]

    def count(mask):
        total = jnp.int32(0)
        for u in range(pool):
            total = total + ((mask >> u) & 1)
        return total

    distinct = (count(has[0]), count(has[1]))
    common = count(both)
    n = jnp.int32(subjects)
    plan = jnp.int32(0)
    for i, (cand, most) in reversed(list(enumerate(plans(subjects)))):
        short = [jnp.maximum(d - cand, 0) for d in distinct]
        fits = jnp.logical_and(short[0] + short[1] <= common, jnp.maximum(short[0], short[1]) <= most)
        n = jnp.where(fits, cand, n)
        plan = jnp.where(fits, i, plan)
    taken = (jnp.maximum(distinct[0] - n, 0), jnp.maximum(distinct[1] - n, 0))
    plan_ref[0] = plan

    take = [jnp.int32(0), jnp.int32(0)]
    seen = jnp.int32(0)
    for u in range(pool):
        bit = (both >> u) & 1
        first = jnp.where(seen < taken[0], bit, 0)
        second = jnp.where(jnp.logical_and(seen >= taken[0], seen < taken[0] + taken[1]), bit, 0)
        take[0] = take[0] | (first << u)
        take[1] = take[1] | (second << u)
        seen = seen + bit
    for p in range(2):
        for k in range(subjects):
            fetch[p, k] = 0
        ahead = jnp.int32(0)
        behind = taken[1 - p]
        for u in range(pool):
            give = (take[1 - p] >> u) & 1
            keep = (((has[p] & ~take[p]) >> u) & 1) * (1 - give)
            spot = jnp.where(give == 1, ahead, behind)
            place[p, u] = spot

            @pl.when(give + keep == 1)
            def _():
                fetch[p, spot] = u

            ahead = ahead + give
            behind = behind + keep
    mine = jnp.where(me == 0, take[0], take[1])
    for k in range(subjects):
        slots_ref[k] = jnp.where(k < n, fetch[me, k], fetch[1 - me, jnp.maximum(k - n, 0)])
    for s in range(subjects):
        u = own_ref[s]
        from_other = ((mine >> u) & 1) == 1
        where_ref[s] = jnp.where(from_other, n + place[1 - me, u], place[me, u])


def tables(me, own, other, pool):
    subjects = own.shape[0]
    smem = pl.BlockSpec(memory_space=pltpu.SMEM)
    return pl.pallas_call(
        table_kernel,
        in_specs=[smem] * 3,
        out_specs=[smem] * 3,
        out_shape=[
            jax.ShapeDtypeStruct((1,), jnp.int32),
            jax.ShapeDtypeStruct((subjects,), jnp.int32),
            jax.ShapeDtypeStruct((subjects,), jnp.int32),
        ],
        scratch_shapes=[
            pltpu.SMEM((2, subjects), jnp.int32),
            pltpu.SMEM((2, pool), jnp.int32),
        ],
    )(me, own, other)


def normalize_kernel(first, turned, slots_ref, series_ref, out_ref, held, done, sem):
    count = held.shape[0]

    def load(i):
        return pltpu.make_async_copy(series_ref.at[slots_ref[first + i]], held.at[i], sem.at[0, i])

    def store(i):
        return pltpu.make_async_copy(done.at[i], out_ref.at[i], sem.at[1, i])

    for i in range(count):
        load(i).start()

    @pl.loop(0, count)
    def _(i):
        load(i).wait()
        values = held[i].astype(jnp.float32)
        center = values - jnp.mean(values, axis=0, keepdims=True)
        spread = jnp.mean(center * center, axis=0, keepdims=True)
        value = center * (1 / jnp.sqrt(spread + EPS))
        done[i] = (value.T if turned else value).astype(jnp.bfloat16)
        store(i).start()

    for i in range(count):
        store(i).wait()


def normalize_slots(series, slots, first, last, turned=False):
    _, frames, rows = series.shape
    shape = (rows, frames) if turned else (frames, rows)
    count = last - first
    any_spec = pl.BlockSpec(memory_space=pl.ANY)
    return pl.pallas_call(
        functools.partial(normalize_kernel, first, turned),
        in_specs=[pl.BlockSpec(memory_space=pltpu.SMEM), any_spec],
        out_specs=any_spec,
        out_shape=jax.ShapeDtypeStruct((count, *shape), jnp.bfloat16),
        scratch_shapes=[
            pltpu.VMEM((count, frames, rows), jnp.bfloat16),
            pltpu.VMEM((count, *shape), jnp.bfloat16),
            pltpu.SemaphoreType.DMA((2, count)),
        ],
        compiler_params=pltpu.CompilerParams(vmem_limit_bytes=VMEM),
        cost_estimate=pl.CostEstimate(
            flops=8 * count * frames * rows,
            bytes_accessed=4 * count * frames * rows,
            transcendentals=0,
        ),
    )(slots, series)


def fisher_kernel(codes, blanks, entries, arrays, has_prev, step, *refs):
    me_ref, labels_ref, where_ref, left_hbm = refs[:4]
    sources = refs[4 : 4 + arrays]
    out_ref, left_ref, buffer, half_ref, tile, blank, todo, left_sem, fetch_sem, tile_sem, blank_sem = refs[
        4 + arrays + has_prev :
    ]
    count = len(codes)
    _, rows, frames = left_ref.shape
    width = buffer.shape[3]
    subjects = where_ref.shape[0]
    me = me_ref[0]
    core = me & 1
    label = labels_ref[me]
    scale = jnp.float32(frames)
    limit = jnp.float32(CLIP * frames)

    def pair_of(code):
        return (me >> 1) ^ code

    def columns(pair, band=slice(None)):
        return out_ref.at[band, pl.ds(pl.multiple_of(pair * (2 * width), 128), 2 * width)]

    total = jnp.int32(0)
    for j, code in enumerate(codes):
        for h in range(2):
            todo[total] = 2 * j + h
            total = total + jnp.where(labels_ref[2 * pair_of(code) + h] == label, 1, 0)

    def start_fetch(i, slot):
        item = todo[i]
        entry = (item & ~1) | jnp.where((item & 1) == core, 0, 1)
        for e, pieces in enumerate(entries):

            @pl.when(entry == e)
            def _():
                at = 0
                for array, first, span in pieces:
                    pltpu.make_async_copy(
                        sources[array].at[pl.ds(first, span)], buffer.at[slot, pl.ds(at, span)], fetch_sem.at[slot]
                    ).start()
                    at += span

    left_copy = pltpu.make_async_copy(left_hbm, left_ref, left_sem.at[0])

    @pl.when(total > 0)
    def _():
        left_copy.start()
        start_fetch(0, 0)

    if blanks:
        blank[...] = jnp.zeros_like(blank)
    empty = []
    for j, code in enumerate(blanks):
        pair = pair_of(code)
        unwanted = jnp.logical_and(labels_ref[2 * pair] != label, labels_ref[2 * pair + 1] != label)
        empty.append((unwanted, pltpu.make_async_copy(blank, columns(pair), blank_sem.at[j])))

        @pl.when(unwanted)
        def _(j=j):
            empty[j][1].start()

    def tile_copy(pair, slot):
        return pltpu.make_async_copy(tile.at[slot], columns(pair), tile_sem.at[slot])

    def code_of(j):
        code = jnp.int32(codes[0])
        for k in range(1, count):
            code = jnp.where(j == k, codes[k], code)
        return code

    chunk = min(256, width)

    @pl.when(total > 0)
    def _():
        left_copy.wait()

    def body(i, pairs):
        slot = i % 2
        item = todo[i]
        j = item >> 1
        h = item & 1
        opens = jnp.logical_or(i == 0, (todo[jnp.maximum(i - 1, 0)] >> 1) != j)
        closes = jnp.logical_or(i == total - 1, (todo[jnp.minimum(i + 1, total - 1)] >> 1) != j)
        pairs = pairs + jnp.where(opens, 1, 0)
        spot = pairs % 2

        @pl.when(i + 1 < total)
        def _():
            start_fetch(i + 1, 1 - slot)

        @pl.when(jnp.logical_and(opens, pairs > 2))
        def _():
            tile_copy(0, spot).wait()

        @pl.when(jnp.logical_and(opens, closes))
        def _():
            tile[spot] = jnp.zeros(tile.shape[1:], jnp.float32)

        pltpu.make_async_copy(buffer.at[slot], buffer.at[slot], fetch_sem.at[slot]).wait()

        @pl.loop(0, rows // step)
        def _(r):
            band = pl.ds(pl.multiple_of(r * step, 16), step)
            for low in range(0, width, chunk):
                high = min(low + chunk, width)
                up = down = None
                for s in range(subjects):
                    k = where_ref[s]
                    corr = jnp.dot(
                        left_ref[k, band, :], buffer[slot, k, :, low:high], preferred_element_type=jnp.float32
                    )
                    corr = jnp.clip(corr, -limit, limit)
                    plus, minus = scale + corr, scale - corr
                    up = plus if up is None else up * plus
                    down = minus if down is None else down * minus
                half_ref[:, low:high] = 0.5 * jnp.log(up / down)
            for half in range(2):

                @pl.when(h == half)
                def _():
                    tile[spot, band, half * width : (half + 1) * width] = half_ref[...]

            @pl.when(closes)
            def _():
                pltpu.make_async_copy(
                    tile.at[spot, band], columns(pair_of(code_of(j)), band), tile_sem.at[spot]
                ).start()

        return pairs

    pairs = lax.fori_loop(0, total, body, jnp.int32(0))

    @pl.when(pairs > 0)
    def _():
        tile_copy(0, pairs % 2).wait()

    @pl.when(pairs > 1)
    def _():
        tile_copy(0, (pairs + 1) % 2).wait()

    for unwanted, copy in empty:

        @pl.when(unwanted)
        def _():
            copy.wait()


def band_rows(rows, longest):
    return next(k for k in range(min(rows, longest), 0, -1) if rows % k == 0 and (k % 16 == 0 or k == rows))


def fisher(me, labels, where, left, pairs, blanks=(), prev=None, longest=192):
    slots, rows, frames = left.shape
    width = rows
    any_spec = pl.BlockSpec(memory_space=pl.ANY)
    smem = pl.BlockSpec(memory_space=pltpu.SMEM)
    arrays, entries = [], []
    for _, *sides in pairs:
        for side in sides:
            entry = []
            for array, first, span in side:
                known = [k for k, x in enumerate(arrays) if x is array]
                if not known:
                    arrays.append(array)
                    known = [len(arrays) - 1]
                entry.append((known[0], first, span))
            entries.append(entry)
    operands = [me, labels, where, left, *arrays] + ([] if prev is None else [prev])
    codes = [pair[0] for pair in pairs]
    return pl.pallas_call(
        functools.partial(
            fisher_kernel, codes, blanks, entries, len(arrays), int(prev is not None), band_rows(rows, longest)
        ),
        in_specs=[smem] * 3 + [any_spec] * (len(operands) - 3),
        out_specs=any_spec,
        out_shape=jax.ShapeDtypeStruct((rows, labels.shape[0] * width), jnp.float32),
        scratch_shapes=[
            pltpu.VMEM((slots, rows, frames), jnp.bfloat16),
            pltpu.VMEM((2, slots, frames, width), jnp.bfloat16),
            pltpu.VMEM((band_rows(rows, longest), width), jnp.float32),
            pltpu.VMEM((2, rows, 2 * width), jnp.float32),
            pltpu.VMEM((rows, 2 * width), jnp.float32),
            pltpu.SMEM((2 * len(codes) + 1,), jnp.int32),
            pltpu.SemaphoreType.DMA((1,)),
            pltpu.SemaphoreType.DMA((2,)),
            pltpu.SemaphoreType.DMA((2,)),
            pltpu.SemaphoreType.DMA((max(len(blanks), 1),)),
        ],
        input_output_aliases={} if prev is None else {len(operands) - 1: 0},
        compiler_params=pltpu.CompilerParams(vmem_limit_bytes=VMEM),
        cost_estimate=pl.CostEstimate(
            flops=2 * rows * width * frames * slots * len(codes),
            bytes_accessed=rows * width * 8 * max(len(codes), len(blanks)),
            transcendentals=rows * width * len(codes),
        ),
    )(*operands)


def pack_kernel(spans, *refs):
    sources, out_ref, held, sem = refs[: len(spans)], refs[-3], refs[-2], refs[-1]
    loads, stores, at = [], [], 0
    for k, span in enumerate(spans):
        place = pl.ds(at, span)
        loads.append(pltpu.make_async_copy(sources[k], held.at[place], sem.at[0, k]))
        stores.append(pltpu.make_async_copy(held.at[place], out_ref.at[place], sem.at[1, k]))
        at += span
    for copy in loads:
        copy.start()
    for load, store in zip(loads, stores):
        load.wait()
        store.start()
    for copy in stores:
        copy.wait()


def pack(*arrays):
    spans = [x.shape[0] for x in arrays]
    shape = (sum(spans), *arrays[0].shape[1:])
    size = 2 * shape[0] * shape[1] * shape[2]
    any_spec = pl.BlockSpec(memory_space=pl.ANY)
    return pl.pallas_call(
        functools.partial(pack_kernel, spans),
        in_specs=[any_spec] * len(spans),
        out_specs=any_spec,
        out_shape=jax.ShapeDtypeStruct(shape, arrays[0].dtype),
        scratch_shapes=[pltpu.VMEM(shape, arrays[0].dtype), pltpu.SemaphoreType.DMA((2, len(spans)))],
        compiler_params=pltpu.CompilerParams(vmem_limit_bytes=VMEM),
        cost_estimate=pl.CostEstimate(flops=0, bytes_accessed=2 * size, transcendentals=0),
    )(*arrays)


def fast(series, subject_ids, net_labels, blocks):
    pool = series.shape[0]
    subjects = subject_ids.shape[0]
    index = lax.axis_index("blk").astype(jnp.int32)
    part = lax.axis_index("parts").astype(jnp.int32)
    other = lax.ppermute(subject_ids, "parts", [(0, 1), (1, 0)])
    plan, slots, where = tables(part[None], subject_ids, other, pool)

    last = (blocks - 1) >> 2
    inner = [i for i in range(blocks) if 0 < i >> 2 < last]
    at_end = jnp.logical_or(index >> 2 == 0, index >> 2 == last)

    def sender(perm):
        return lambda x: lax.ppermute(x, "blk", perm)

    core = sender([(i, i ^ 1) for i in range(blocks)])
    along_x = sender([(i, i ^ 2) for i in range(blocks)])
    along_z = sender([(i, i ^ 4) for i in range(blocks)])
    middle = sender([(i, i ^ 12) for i in inner])
    outward = sender([(i, i ^ 4) for i in inner])

    def branch(n, m):
        half = m
        together = lax.optimization_barrier

        def along_y(*arrays):
            if not m:
                return None
            joint = jnp.concatenate([x[:m] for x in arrays]) if len(arrays) > 1 else arrays[0][:m]
            return lax.ppermute(joint, "parts", [(0, 1), (1, 0)])

        def twin(x):
            return None if x is None else core(x)

        def fit(*pieces):
            return [p for p in pieces if p[2]]

        def run(series, slots, where, net_labels):
            step = functools.partial(fisher, index[None], net_labels, where)

            def pair(code, a, y, k, both, y_s):
                return code, fit((a, 0, n), (y, k * m, m)), fit((both, k * n, n), (y_s, k * m, m))

            own = normalize_slots(series, slots, 0, n)
            r1, mid, x0, own_s = along_z(own), middle(own), along_x(own), core(own)
            taken = normalize_slots(series, slots, n, n + m) if m else None
            taken_s = twin(taken)
            left = normalize_slots(series, slots, 0, n + m, turned=True)
            r1, mid, x0, own_s, taken, taken_s, left = together((r1, mid, x0, own_s, taken, taken_s, left))

            e2, b2, x1, y1 = outward(mid), middle(r1), along_x(r1), along_y(r1, x0)
            joint2 = pack(r1, x0)
            out = step(
                left,
                [(0, fit((own, 0, n), (taken, 0, m)), fit((own_s, 0, n), (taken_s, 0, m)))],
                blanks=tuple(range(blocks // 2)),
                longest=64,
            )
            r2 = jnp.where(at_end, e2, b2)
            r2, x1, y1, joint2, out = together((r2, x1, y1, joint2, out))

            r3, x2, y2, core2, y1_s = along_z(r2), along_x(r2), along_y(r2, x1), core(joint2), twin(y1)
            joint3 = pack(r2, x1)
            r3, x2, y2, core2, y1_s, joint3 = together((r3, x2, y2, core2, y1_s, joint3))

            x3, rest, y3 = along_x(r3[:half]), along_z(x2[half:]), along_y(r3, x2)
            core3, y2_s = core(joint3), twin(y2)
            joint4 = pack(r3, x2)
            out = step(
                left,
                [pair(2, r1, y1, 0, core2, y1_s), pair(1, x0, y1, 1, core2, y1_s)],
                prev=out,
                longest=64,
            )
            rest, x3, y3, core3, y2_s, joint4, out = together((rest, x3, y3, core3, y2_s, joint4, out))

            y4, core4, y3_s, x3_s, rest_s = along_y(x3), core(joint4), twin(y3), core(x3), core(rest)
            out = step(
                left,
                [pair(4, r2, y2, 0, core3, y2_s), pair(3, x1, y2, 1, core3, y2_s)],
                prev=out,
            )
            y4, core4, y3_s, x3_s, rest_s, out = together((y4, core4, y3_s, x3_s, rest_s, out))

            y4_s = twin(y4)
            mine = fit((x3, 0, half), (rest, 0, n - half), (y4, 0, m))
            sibling = fit((x3_s, 0, half), (rest_s, 0, n - half), (y4_s, 0, m))
            return step(
                left,
                [
                    pair(6, r3, y3, 0, core4, y3_s),
                    pair(5, x2, y3, 1, core4, y3_s),
                    (7, mine, sibling),
                ],
                prev=out,
                longest=384,
            )

        return run

    def unshared(series, slots, where, net_labels):
        own = normalize_slots(series, slots, 0, subjects)
        left = normalize_slots(series, slots, 0, subjects, turned=True)
        r1 = along_z(own)
        r2 = jnp.where(at_end, outward(middle(own)), middle(r1))
        column = [own, r1, r2, along_z(r2)]
        mine = column + [along_x(x) for x in column]
        codes = [0, 2, 4, 6, 1, 3, 5, 7]

        def whole(x):
            return [(x, 0, subjects)]

        pairs = [(code, whole(x), whole(core(x))) for code, x in zip(codes, mine)]
        return fisher(
            index[None], net_labels, where, left, pairs, blanks=tuple(range(blocks // 2)), longest=64
        )

    runs = [branch(n, m) if m else unshared for n, m in plans(subjects)]
    return lax.switch(plan[0], runs, series, slots, where, net_labels)


def general(series, subject_ids, net_labels, block):
    chosen = jnp.take(series, subject_ids, axis=0).astype(jnp.float32)
    center = chosen - jnp.mean(chosen, axis=1, keepdims=True)
    spread = jnp.mean(center * center, axis=1, keepdims=True)
    left = (center / jnp.sqrt(spread + EPS)).astype(jnp.bfloat16)
    subjects, frames, rows = left.shape
    right = lax.all_gather(left, "blk", axis=2, tiled=True)
    row_labels = jnp.repeat(net_labels, block)
    own_labels = lax.dynamic_slice_in_dim(row_labels, lax.axis_index("blk") * rows, rows)
    up = down = jnp.float32(1)
    for s in range(subjects):
        corr = lax.dot_general(
            left[s], right[s], (((0,), (0,)), ((), ())), preferred_element_type=jnp.float32
        )
        corr = jnp.clip(corr / frames, -CLIP, CLIP)
        up, down = up * (1 + corr), down * (1 - corr)
    total = 0.5 * jnp.log(up / down)
    return jnp.where(own_labels[:, None] == row_labels[None, :], total, jnp.zeros_like(total))


def solution(mesh):
    parts, devices = mesh.shape["parts"], mesh.shape["blk"]

    def on_device(series, subject_ids, net_labels):
        blocks = net_labels.shape[0]
        rows = series.shape[2]
        grid = 4 * 2 * 2
        if parts == 2 and devices == blocks == grid and 2 * rows % 128 == 0:
            return fast(series, subject_ids, net_labels, blocks)
        return general(series, subject_ids, net_labels, rows * devices // blocks)

    return jax.shard_map(
        on_device,
        mesh=mesh,
        in_specs=(P(None, None, "blk"), P("parts"), P()),
        out_specs=P(("parts", "blk"), None),
        check_vma=False,
    )
```

```python
import functools

import jax
import jax.numpy as jnp
from jax import lax
from jax.experimental import pallas as pl
from jax.experimental.pallas import tpu as pltpu
from jax.sharding import PartitionSpec as P

CLIP = 0.999
EPS = 1e-05
VMEM = 56 * 2**20


def plans(subjects):
    n = subjects * 5 // 8
    return [(n, subjects - n - 1), (n + 1, subjects - n - 1), (subjects, 0)]


def table_kernel(me_ref, own_ref, other_ref, plan_ref, slots_ref, where_ref, fetch, place):
    subjects = own_ref.shape[0]
    pool = place.shape[1]
    me = me_ref[0]
    one = jnp.int32(1)
    own = jnp.int32(0)
    other = jnp.int32(0)
    for s in range(subjects):
        own = own | (one << own_ref[s])
        other = other | (one << other_ref[s])
    has = (jnp.where(me == 0, own, other), jnp.where(me == 0, other, own))
    both = has[0] & has[1]

    def count(mask):
        total = jnp.int32(0)
        for u in range(pool):
            total = total + ((mask >> u) & 1)
        return total

    distinct = (count(has[0]), count(has[1]))
    common = count(both)
    n = jnp.int32(subjects)
    plan = jnp.int32(0)
    for i, (cand, most) in reversed(list(enumerate(plans(subjects)))):
        short = [jnp.maximum(d - cand, 0) for d in distinct]
        fits = jnp.logical_and(short[0] + short[1] <= common, jnp.maximum(short[0], short[1]) <= most)
        n = jnp.where(fits, cand, n)
        plan = jnp.where(fits, i, plan)
    taken = (jnp.maximum(distinct[0] - n, 0), jnp.maximum(distinct[1] - n, 0))
    plan_ref[0] = plan

    take = [jnp.int32(0), jnp.int32(0)]
    seen = jnp.int32(0)
    for u in range(pool):
        bit = (both >> u) & 1
        first = jnp.where(seen < taken[0], bit, 0)
        second = jnp.where(jnp.logical_and(seen >= taken[0], seen < taken[0] + taken[1]), bit, 0)
        take[0] = take[0] | (first << u)
        take[1] = take[1] | (second << u)
        seen = seen + bit
    for p in range(2):
        for k in range(subjects):
            fetch[p, k] = 0
        ahead = jnp.int32(0)
        behind = taken[1 - p]
        for u in range(pool):
            give = (take[1 - p] >> u) & 1
            keep = (((has[p] & ~take[p]) >> u) & 1) * (1 - give)
            spot = jnp.where(give == 1, ahead, behind)
            place[p, u] = spot

            @pl.when(give + keep == 1)
            def _():
                fetch[p, spot] = u

            ahead = ahead + give
            behind = behind + keep
    mine = jnp.where(me == 0, take[0], take[1])
    for k in range(subjects):
        slots_ref[k] = jnp.where(k < n, fetch[me, k], fetch[1 - me, jnp.maximum(k - n, 0)])
    for s in range(subjects):
        u = own_ref[s]
        from_other = ((mine >> u) & 1) == 1
        where_ref[s] = jnp.where(from_other, n + place[1 - me, u], place[me, u])


def tables(me, own, other, pool):
    subjects = own.shape[0]
    smem = pl.BlockSpec(memory_space=pltpu.SMEM)
    return pl.pallas_call(
        table_kernel,
        in_specs=[smem] * 3,
        out_specs=[smem] * 3,
        out_shape=[
            jax.ShapeDtypeStruct((1,), jnp.int32),
            jax.ShapeDtypeStruct((subjects,), jnp.int32),
            jax.ShapeDtypeStruct((subjects,), jnp.int32),
        ],
        scratch_shapes=[
            pltpu.SMEM((2, subjects), jnp.int32),
            pltpu.SMEM((2, pool), jnp.int32),
        ],
    )(me, own, other)


def normalize_kernel(first, turned, slots_ref, series_ref, out_ref, held, done, sem):
    count = held.shape[0]

    def load(i):
        return pltpu.make_async_copy(series_ref.at[slots_ref[first + i]], held.at[i], sem.at[0, i])

    def store(i):
        return pltpu.make_async_copy(done.at[i], out_ref.at[i], sem.at[1, i])

    for i in range(count):
        load(i).start()

    @pl.loop(0, count)
    def _(i):
        load(i).wait()
        values = held[i].astype(jnp.float32)
        center = values - jnp.mean(values, axis=0, keepdims=True)
        spread = jnp.mean(center * center, axis=0, keepdims=True)
        value = center * (1 / jnp.sqrt(spread + EPS))
        done[i] = (value.T if turned else value).astype(jnp.bfloat16)
        store(i).start()

    for i in range(count):
        store(i).wait()


def normalize_slots(series, slots, first, last, turned=False):
    _, frames, rows = series.shape
    shape = (rows, frames) if turned else (frames, rows)
    count = last - first
    any_spec = pl.BlockSpec(memory_space=pl.ANY)
    return pl.pallas_call(
        functools.partial(normalize_kernel, first, turned),
        in_specs=[pl.BlockSpec(memory_space=pltpu.SMEM), any_spec],
        out_specs=any_spec,
        out_shape=jax.ShapeDtypeStruct((count, *shape), jnp.bfloat16),
        scratch_shapes=[
            pltpu.VMEM((count, frames, rows), jnp.bfloat16),
            pltpu.VMEM((count, *shape), jnp.bfloat16),
            pltpu.SemaphoreType.DMA((2, count)),
        ],
        compiler_params=pltpu.CompilerParams(vmem_limit_bytes=VMEM),
        cost_estimate=pl.CostEstimate(
            flops=8 * count * frames * rows,
            bytes_accessed=4 * count * frames * rows,
            transcendentals=0,
        ),
    )(slots, series)


def fisher_kernel(codes, blanks, entries, arrays, has_prev, step, *refs):
    me_ref, labels_ref, where_ref, left_hbm = refs[:4]
    sources = refs[4 : 4 + arrays]
    out_ref, left_ref, buffer, half_ref, tile, blank, todo, left_sem, fetch_sem, tile_sem, blank_sem = refs[
        4 + arrays + has_prev :
    ]
    count = len(codes)
    _, rows, frames = left_ref.shape
    width = buffer.shape[3]
    subjects = where_ref.shape[0]
    me = me_ref[0]
    core = me & 1
    label = labels_ref[me]
    scale = jnp.float32(frames)
    limit = jnp.float32(CLIP * frames)

    def pair_of(code):
        return (me >> 1) ^ code

    def columns(pair, band=slice(None)):
        return out_ref.at[band, pl.ds(pl.multiple_of(pair * (2 * width), 128), 2 * width)]

    total = jnp.int32(0)
    for j, code in enumerate(codes):
        for h in range(2):
            todo[total] = 2 * j + h
            total = total + jnp.where(labels_ref[2 * pair_of(code) + h] == label, 1, 0)

    def start_fetch(i, slot):
        item = todo[i]
        entry = (item & ~1) | jnp.where((item & 1) == core, 0, 1)
        for e, pieces in enumerate(entries):

            @pl.when(entry == e)
            def _():
                at = 0
                for array, first, span in pieces:
                    pltpu.make_async_copy(
                        sources[array].at[pl.ds(first, span)], buffer.at[slot, pl.ds(at, span)], fetch_sem.at[slot]
                    ).start()
                    at += span

    left_copy = pltpu.make_async_copy(left_hbm, left_ref, left_sem.at[0])

    @pl.when(total > 0)
    def _():
        left_copy.start()
        start_fetch(0, 0)

    if blanks:
        blank[...] = jnp.zeros_like(blank)
    empty = []
    for j, code in enumerate(blanks):
        pair = pair_of(code)
        unwanted = jnp.logical_and(labels_ref[2 * pair] != label, labels_ref[2 * pair + 1] != label)
        empty.append((unwanted, pltpu.make_async_copy(blank, columns(pair), blank_sem.at[j])))

        @pl.when(unwanted)
        def _(j=j):
            empty[j][1].start()

    def tile_copy(pair, slot):
        return pltpu.make_async_copy(tile.at[slot], columns(pair), tile_sem.at[slot])

    def code_of(j):
        code = jnp.int32(codes[0])
        for k in range(1, count):
            code = jnp.where(j == k, codes[k], code)
        return code

    chunk = min(256, width)

    @pl.when(total > 0)
    def _():
        left_copy.wait()

    def body(i, pairs):
        slot = i % 2
        item = todo[i]
        j = item >> 1
        h = item & 1
        opens = jnp.logical_or(i == 0, (todo[jnp.maximum(i - 1, 0)] >> 1) != j)
        closes = jnp.logical_or(i == total - 1, (todo[jnp.minimum(i + 1, total - 1)] >> 1) != j)
        pairs = pairs + jnp.where(opens, 1, 0)
        spot = pairs % 2

        @pl.when(i + 1 < total)
        def _():
            start_fetch(i + 1, 1 - slot)

        @pl.when(jnp.logical_and(opens, pairs > 2))
        def _():
            tile_copy(0, spot).wait()

        @pl.when(jnp.logical_and(opens, closes))
        def _():
            tile[spot] = jnp.zeros(tile.shape[1:], jnp.float32)

        pltpu.make_async_copy(buffer.at[slot], buffer.at[slot], fetch_sem.at[slot]).wait()

        @pl.loop(0, rows // step)
        def _(r):
            band = pl.ds(pl.multiple_of(r * step, 16), step)
            for low in range(0, width, chunk):
                high = min(low + chunk, width)
                up = down = None
                for s in range(subjects):
                    k = where_ref[s]
                    corr = jnp.dot(
                        left_ref[k, band, :], buffer[slot, k, :, low:high], preferred_element_type=jnp.float32
                    )
                    corr = jnp.clip(corr, -limit, limit)
                    plus, minus = scale + corr, scale - corr
                    up = plus if up is None else up * plus
                    down = minus if down is None else down * minus
                half_ref[:, low:high] = 0.5 * jnp.log(up / down)
            for half in range(2):

                @pl.when(h == half)
                def _():
                    tile[spot, band, half * width : (half + 1) * width] = half_ref[...]

            @pl.when(closes)
            def _():
                pltpu.make_async_copy(
                    tile.at[spot, band], columns(pair_of(code_of(j)), band), tile_sem.at[spot]
                ).start()

        return pairs

    pairs = lax.fori_loop(0, total, body, jnp.int32(0))

    @pl.when(pairs > 0)
    def _():
        tile_copy(0, pairs % 2).wait()

    @pl.when(pairs > 1)
    def _():
        tile_copy(0, (pairs + 1) % 2).wait()

    for unwanted, copy in empty:

        @pl.when(unwanted)
        def _():
            copy.wait()


def band_rows(rows, longest):
    return next(k for k in range(min(rows, longest), 0, -1) if rows % k == 0 and (k % 16 == 0 or k == rows))


def fisher(me, labels, where, left, pairs, blanks=(), prev=None, longest=192):
    slots, rows, frames = left.shape
    width = rows
    any_spec = pl.BlockSpec(memory_space=pl.ANY)
    smem = pl.BlockSpec(memory_space=pltpu.SMEM)
    arrays, entries = [], []
    for _, *sides in pairs:
        for side in sides:
            entry = []
            for array, first, span in side:
                known = [k for k, x in enumerate(arrays) if x is array]
                if not known:
                    arrays.append(array)
                    known = [len(arrays) - 1]
                entry.append((known[0], first, span))
            entries.append(entry)
    operands = [me, labels, where, left, *arrays] + ([] if prev is None else [prev])
    codes = [pair[0] for pair in pairs]
    return pl.pallas_call(
        functools.partial(
            fisher_kernel, codes, blanks, entries, len(arrays), int(prev is not None), band_rows(rows, longest)
        ),
        in_specs=[smem] * 3 + [any_spec] * (len(operands) - 3),
        out_specs=any_spec,
        out_shape=jax.ShapeDtypeStruct((rows, labels.shape[0] * width), jnp.float32),
        scratch_shapes=[
            pltpu.VMEM((slots, rows, frames), jnp.bfloat16),
            pltpu.VMEM((2, slots, frames, width), jnp.bfloat16),
            pltpu.VMEM((band_rows(rows, longest), width), jnp.float32),
            pltpu.VMEM((2, rows, 2 * width), jnp.float32),
            pltpu.VMEM((rows, 2 * width), jnp.float32),
            pltpu.SMEM((2 * len(codes) + 1,), jnp.int32),
            pltpu.SemaphoreType.DMA((1,)),
            pltpu.SemaphoreType.DMA((2,)),
            pltpu.SemaphoreType.DMA((2,)),
            pltpu.SemaphoreType.DMA((max(len(blanks), 1),)),
        ],
        input_output_aliases={} if prev is None else {len(operands) - 1: 0},
        compiler_params=pltpu.CompilerParams(vmem_limit_bytes=VMEM),
        cost_estimate=pl.CostEstimate(
            flops=2 * rows * width * frames * slots * len(codes),
            bytes_accessed=rows * width * 8 * max(len(codes), len(blanks)),
            transcendentals=rows * width * len(codes),
        ),
    )(*operands)


def pack_kernel(spans, *refs):
    sources, out_ref, held, sem = refs[: len(spans)], refs[-3], refs[-2], refs[-1]
    loads, stores, at = [], [], 0
    for k, span in enumerate(spans):
        place = pl.ds(at, span)
        loads.append(pltpu.make_async_copy(sources[k], held.at[place], sem.at[0, k]))
        stores.append(pltpu.make_async_copy(held.at[place], out_ref.at[place], sem.at[1, k]))
        at += span
    for copy in loads:
        copy.start()
    for load, store in zip(loads, stores):
        load.wait()
        store.start()
    for copy in stores:
        copy.wait()


def pack(*arrays):
    spans = [x.shape[0] for x in arrays]
    shape = (sum(spans), *arrays[0].shape[1:])
    size = 2 * shape[0] * shape[1] * shape[2]
    any_spec = pl.BlockSpec(memory_space=pl.ANY)
    return pl.pallas_call(
        functools.partial(pack_kernel, spans),
        in_specs=[any_spec] * len(spans),
        out_specs=any_spec,
        out_shape=jax.ShapeDtypeStruct(shape, arrays[0].dtype),
        scratch_shapes=[pltpu.VMEM(shape, arrays[0].dtype), pltpu.SemaphoreType.DMA((2, len(spans)))],
        compiler_params=pltpu.CompilerParams(vmem_limit_bytes=VMEM),
        cost_estimate=pl.CostEstimate(flops=0, bytes_accessed=2 * size, transcendentals=0),
    )(*arrays)


def fast(series, subject_ids, net_labels, blocks):
    pool = series.shape[0]
    subjects = subject_ids.shape[0]
    index = lax.axis_index("blk").astype(jnp.int32)
    part = lax.axis_index("parts").astype(jnp.int32)
    other = lax.ppermute(subject_ids, "parts", [(0, 1), (1, 0)])
    plan, slots, where = tables(part[None], subject_ids, other, pool)

    last = (blocks - 1) >> 2
    inner = [i for i in range(blocks) if 0 < i >> 2 < last]
    at_end = jnp.logical_or(index >> 2 == 0, index >> 2 == last)

    def sender(perm):
        return lambda x: lax.ppermute(x, "blk", perm)

    core = sender([(i, i ^ 1) for i in range(blocks)])
    along_x = sender([(i, i ^ 2) for i in range(blocks)])
    along_z = sender([(i, i ^ 4) for i in range(blocks)])
    middle = sender([(i, i ^ 12) for i in inner])
    outward = sender([(i, i ^ 4) for i in inner])

    def branch(n, m):
        half = m
        together = lax.optimization_barrier

        def along_y(*arrays):
            if not m:
                return None
            joint = jnp.concatenate([x[:m] for x in arrays]) if len(arrays) > 1 else arrays[0][:m]
            return lax.ppermute(joint, "parts", [(0, 1), (1, 0)])

        def twin(x):
            return None if x is None else core(x)

        def fit(*pieces):
            return [p for p in pieces if p[2]]

        def run(series, slots, where, net_labels):
            step = functools.partial(fisher, index[None], net_labels, where)

            def pair(code, a, y, k, both, y_s):
                return code, fit((a, 0, n), (y, k * m, m)), fit((both, k * n, n), (y_s, k * m, m))

            own = normalize_slots(series, slots, 0, n)
            r1, mid, x0, own_s = along_z(own), middle(own), along_x(own), core(own)
            taken = normalize_slots(series, slots, n, n + m) if m else None
            taken_s = twin(taken)
            left = normalize_slots(series, slots, 0, n + m, turned=True)
            r1, mid, x0, own_s, taken, taken_s, left = together((r1, mid, x0, own_s, taken, taken_s, left))

            e2, b2, x1, y1 = outward(mid), middle(r1), along_x(r1), along_y(r1, x0)
            joint2 = pack(r1, x0)
            out = step(
                left,
                [(0, fit((own, 0, n), (taken, 0, m)), fit((own_s, 0, n), (taken_s, 0, m)))],
                blanks=tuple(range(blocks // 2)),
                longest=64,
            )
            r2 = jnp.where(at_end, e2, b2)
            r2, x1, y1, joint2, out = together((r2, x1, y1, joint2, out))

            r3, x2, y2, core2, y1_s = along_z(r2), along_x(r2), along_y(r2, x1), core(joint2), twin(y1)
            joint3 = pack(r2, x1)
            r3, x2, y2, core2, y1_s, joint3 = together((r3, x2, y2, core2, y1_s, joint3))

            x3, rest, y3 = along_x(r3[:half]), along_z(x2[half:]), along_y(r3, x2)
            core3, y2_s = core(joint3), twin(y2)
            joint4 = pack(r3, x2)
            out = step(
                left,
                [pair(2, r1, y1, 0, core2, y1_s), pair(1, x0, y1, 1, core2, y1_s)],
                prev=out,
            )
            rest, x3, y3, core3, y2_s, joint4, out = together((rest, x3, y3, core3, y2_s, joint4, out))

            y4, core4, y3_s, x3_s, rest_s = along_y(x3), core(joint4), twin(y3), core(x3), core(rest)
            out = step(
                left,
                [pair(4, r2, y2, 0, core3, y2_s), pair(3, x1, y2, 1, core3, y2_s)],
                prev=out,
                longest=384,
            )
            y4, core4, y3_s, x3_s, rest_s, out = together((y4, core4, y3_s, x3_s, rest_s, out))

            y4_s = twin(y4)
            mine = fit((x3, 0, half), (rest, 0, n - half), (y4, 0, m))
            sibling = fit((x3_s, 0, half), (rest_s, 0, n - half), (y4_s, 0, m))
            return step(
                left,
                [
                    pair(6, r3, y3, 0, core4, y3_s),
                    pair(5, x2, y3, 1, core4, y3_s),
                    (7, mine, sibling),
                ],
                prev=out,
                longest=384,
            )

        return run

    def unshared(series, slots, where, net_labels):
        own = normalize_slots(series, slots, 0, subjects)
        left = normalize_slots(series, slots, 0, subjects, turned=True)
        r1 = along_z(own)
        r2 = jnp.where(at_end, outward(middle(own)), middle(r1))
        column = [own, r1, r2, along_z(r2)]
        mine = column + [along_x(x) for x in column]
        codes = [0, 2, 4, 6, 1, 3, 5, 7]

        def whole(x):
            return [(x, 0, subjects)]

        pairs = [(code, whole(x), whole(core(x))) for code, x in zip(codes, mine)]
        return fisher(
            index[None], net_labels, where, left, pairs, blanks=tuple(range(blocks // 2)), longest=64
        )

    runs = [branch(n, m) if m else unshared for n, m in plans(subjects)]
    return lax.switch(plan[0], runs, series, slots, where, net_labels)


def general(series, subject_ids, net_labels, block):
    chosen = jnp.take(series, subject_ids, axis=0).astype(jnp.float32)
    center = chosen - jnp.mean(chosen, axis=1, keepdims=True)
    spread = jnp.mean(center * center, axis=1, keepdims=True)
    left = (center / jnp.sqrt(spread + EPS)).astype(jnp.bfloat16)
    subjects, frames, rows = left.shape
    right = lax.all_gather(left, "blk", axis=2, tiled=True)
    row_labels = jnp.repeat(net_labels, block)
    own_labels = lax.dynamic_slice_in_dim(row_labels, lax.axis_index("blk") * rows, rows)
    up = down = jnp.float32(1)
    for s in range(subjects):
        corr = lax.dot_general(
            left[s], right[s], (((0,), (0,)), ((), ())), preferred_element_type=jnp.float32
        )
        corr = jnp.clip(corr / frames, -CLIP, CLIP)
        up, down = up * (1 + corr), down * (1 - corr)
    total = 0.5 * jnp.log(up / down)
    return jnp.where(own_labels[:, None] == row_labels[None, :], total, jnp.zeros_like(total))


def solution(mesh):
    parts, devices = mesh.shape["parts"], mesh.shape["blk"]

    def on_device(series, subject_ids, net_labels):
        blocks = net_labels.shape[0]
        rows = series.shape[2]
        grid = 4 * 2 * 2
        if parts == 2 and devices == blocks == grid and 2 * rows % 128 == 0:
            return fast(series, subject_ids, net_labels, blocks)
        return general(series, subject_ids, net_labels, rows * devices // blocks)

    return jax.shard_map(
        on_device,
        mesh=mesh,
        in_specs=(P(None, None, "blk"), P("parts"), P()),
        out_specs=P(("parts", "blk"), None),
        check_vma=False,
    )
```
